256 devices in a mesh: path: 4 (over z_lo), tensor: 8 (over y, core), problem: 8 (over x, z_hi).
Axes of the slice: x: 4, y: 4, z: 8 (z_hi: 2, z_lo: 4; z = z_hi * 4 + z_lo), core: 2. Of those that a mesh axis runs over, the one named last changes fastest.
Arguments:
- decode_in: bfloat16 [64, 4, 4096], P(('problem', 'path')), parts along dimension 0, may hold values from -6 to 6
- path_embed: bfloat16 [8, 4096], P('path'), may hold values from -6 to 6
- summary_in: bfloat16 [2048, 4096], P(('problem', 'path', 'tensor')), parts along dimension 0, may hold values from -6 to 6
- norm_gain: bfloat16 [4096], replicated, may hold values from 0.099609375 to 1.8984375
- query_gain: bfloat16 [128], replicated, may hold values from 0.099609375 to 1.8984375
- key_norm_gain: bfloat16 [128], replicated, may hold values from 1 to 4
- w_query: bfloat16 [4096, 4096], P(None, 'tensor'), may hold values from -0.09375 to 0.09375
- key_weight: bfloat16 [4096, 1024], P(None, 'tensor'), may hold values from -0.09375 to 0.09375
- w_value: bfloat16 [4096, 1024], P(None, 'tensor'), may hold values from -0.09375 to 0.09375
- w_out: bfloat16 [4096, 4096], P('tensor'), may hold values from -0.09375 to 0.09375
- key_cache: bfloat16 [64, 2048, 1024], P(('problem', 'path'), None, 'tensor'), parts along dimension 0, may hold values from -240 to 240
- value_cache: bfloat16 [64, 2048, 1024], P(('problem', 'path'), None, 'tensor'), parts along dimension 0, may hold values from -6 to 6
- lengths: int32 [64], P('problem'), parts along dimension 0, may hold values from 512 to 2044, as said below
Outputs:
- decode_out: bfloat16 [64, 4, 4096], P(('problem', 'path'), None, 'tensor'), parts along dimension 0
- summary_out: bfloat16 [2048, 4096], P(('problem', 'path', 'tensor')), parts along dimension 0
The draws below stay inside these ranges and needn't reach their ends.
There are 8 independent parts, one for each index of `problem`. The reference program is written for one: setup_inputs(seed, part) draws one part's arguments, and reference() takes and returns one part's arrays. A program takes and returns all parts, laid end to end along the dimension named above; an argument that names none is the same for every part. Nothing has to cross between parts.
Inputs may be any that keep to these rules, and one draw needn't show every extreme that they name: `lengths`: every path has at least one valid entry; at least one path has exactly 2044 and at least one exactly 512.
All inputs are finite; a program needn't handle non-finite values.
Results may differ from the reference program's by a relative error of at most 0.027.
The reference program's roundings to bfloat16 on the way count: a program that leaves them out, or rounds other values in their place, can miss the bound.
Values may be sent and summed in bfloat16 or wider, within the bound.
No kernel may reach another device: no remote copies, remote signals or barrier semaphores. Data moves between devices by JAX's collectives and lax.ppermute only.
A program may use at most 128 MiB of HBM per device.

```python
import math
import jax
import jax.numpy as jnp
from jax import lax

D = 4096
HEADS = 32
KEY_VALUE_HEADS = 8
HEAD_SIZE = 128
CACHE = 2048
SUMMARY_TOKENS = 256
STEPS = 4
PATHS = 8


def draw_key_cache(key, part):
    key = jax.random.fold_in(key, 5)
    key_one = jax.random.fold_in(key, 0)
    entries = jax.random.normal(key_one, (PATHS, CACHE, KEY_VALUE_HEADS, HEAD_SIZE), jnp.float32)
    entries = jnp.clip(entries * 2.5, -15.0, 15.0)
    return entries.reshape(PATHS, CACHE, KEY_VALUE_HEADS * HEAD_SIZE).astype(jnp.bfloat16)


def draw_lengths(key, part):
    key = jax.random.fold_in(key, 11)
    key_one, key_two = jax.random.split(key)
    chosen = jax.random.randint(key_one, (PATHS,), CACHE // 4, CACHE - STEPS + 1)
    shuffled = jax.random.permutation(key_two, PATHS)
    chosen = jnp.where(shuffled == 0, CACHE - STEPS, chosen)
    chosen = jnp.where(shuffled == 1, CACHE // 4, chosen)
    return chosen.astype(jnp.int32)


def steps_of(rng, dims, cuts, smallest, top_value):
    level = 1.0
    for position, shards_of in cuts:
        heights = jax.random.uniform(jax.random.fold_in(jax.random.fold_in(rng, 6), position), (shards_of,), jnp.float32, smallest / len(cuts), top_value / len(cuts))
        level = level * jnp.repeat(jnp.exp(heights), dims[position] // shards_of).reshape((-1,) + (1,) * (len(dims) - 1 - position))
    return level


def bell_draw(rng, extent, spread, bound, shards=(), kind=jnp.bfloat16):
    result = jax.random.normal(rng, extent, jnp.float32) * spread
    if len(shards) > 0:
        result = steps_of(rng, extent, shards, -0.22, 0.18) * result
    return jnp.clip(result, min=-bound, max=bound).astype(kind)


def setup_inputs(seed: int = 0, part: int = 0) -> dict:
    splits = jax.random.split(jax.random.key(seed), 14)
    own_keys = jax.random.split(jax.random.fold_in(splits[13], part), 14)
    decode_in = bell_draw(own_keys[0], (PATHS, STEPS, D), 1.0, 6.0, ((0, 4),))
    path_embed = bell_draw(splits[1], (PATHS, D), 1.0, 6.0, ((0, 4),))
    summary_in = bell_draw(own_keys[2], (SUMMARY_TOKENS, D), 1.0, 6.0, ((0, 32),))
    norm_gain = jnp.clip(1.0 + 0.18 * jax.random.normal(splits[3], (D,), jnp.float32), 0.099609375, 1.8984375).astype(jnp.bfloat16)
    query_gain = jnp.clip(1.0 + 0.18 * jax.random.normal(splits[4], (HEAD_SIZE,), jnp.float32), 0.099609375, 1.8984375).astype(jnp.bfloat16)
    key_norm_gain = jnp.clip(jnp.exp(jax.random.uniform(splits[5], (HEAD_SIZE,), jnp.float32, math.log(1.0), math.log(4.0))), 1.0, 4.0).astype(jnp.bfloat16)
    w_query = bell_draw(splits[6], (D, HEADS * HEAD_SIZE), D ** -0.5, 0.09375, ((1, 8),))
    key_weight = bell_draw(splits[7], (D, KEY_VALUE_HEADS * HEAD_SIZE), D ** -0.5, 0.09375, ((1, 8),))
    w_value = bell_draw(splits[8], (D, KEY_VALUE_HEADS * HEAD_SIZE), D ** -0.5, 0.09375, ((1, 8),))
    w_out = bell_draw(splits[9], (HEADS * HEAD_SIZE, D), (HEADS * HEAD_SIZE) ** -0.5, 0.09375, ((0, 8),))
    key_cache = draw_key_cache(jax.random.fold_in(jax.random.fold_in(splits[13], part), 71), part)
    value_cache = bell_draw(own_keys[11], (PATHS, CACHE, KEY_VALUE_HEADS * HEAD_SIZE), 1.0, 6.0, ((0, 4), (2, 8)))
    lengths = draw_lengths(jax.random.fold_in(jax.random.fold_in(splits[13], part), 71), part)
    return {"decode_in": decode_in, "path_embed": path_embed, "summary_in": summary_in, "norm_gain": norm_gain, "query_gain": query_gain, "key_norm_gain": key_norm_gain, "w_query": w_query, "key_weight": key_weight, "w_value": w_value, "w_out": w_out, "key_cache": key_cache, "value_cache": value_cache, "lengths": lengths}


epsilon = 1e-06
rope_base = 1000000.0

def normalize(rows, gain):
    factor = lax.rsqrt(lax.optimization_barrier(jnp.mean(rows * rows, axis=-1, keepdims=True)) + epsilon)
    return rows * factor * gain.astype(rows.dtype)

def rotate(vectors, positions):
    head_width = vectors.shape[-1]
    half_width = head_width // 2
    exponent = jnp.arange(half_width).astype(vectors.dtype) * (2.0 / head_width)
    freqs = jnp.exp(-math.log(rope_base) * exponent)
    angles = positions.astype(vectors.dtype)[:, None, None] * freqs
    cosine = jnp.cos(angles)
    sine = jnp.sin(angles)
    leading = vectors[..., :half_width]
    trailing = vectors[..., half_width:]
    return jnp.concatenate([leading * cosine - trailing * sine, trailing * cosine + leading * sine], axis=-1)

def project_rows(normed, weight, gain, positions):
    projected = jnp.dot(normed, weight, preferred_element_type=jnp.float32)
    projected = projected.reshape(projected.shape[0], -1, gain.shape[0])
    return rotate(normalize(projected, gain), positions).astype(jnp.bfloat16)

def attend(query, key_rows, value_rows, allowed):
    scores = jnp.einsum('rgd,nd->rgn', query.astype(jnp.float32), key_rows.astype(jnp.float32)) / math.sqrt(query.shape[-1])
    scores = jnp.where(allowed[:, None, :], scores, -jnp.inf)
    peak = lax.optimization_barrier(jnp.max(scores, axis=-1, keepdims=True))
    weights = jnp.exp(scores - peak)
    totals = lax.optimization_barrier(jnp.sum(weights, axis=-1))
    rounded = weights.astype(jnp.bfloat16).astype(jnp.float32)
    mixture = jnp.einsum('rgn,nd->rgd', rounded, value_rows.astype(jnp.float32))
    return mixture / totals[..., None]

def reference(decode_in, path_embed, summary_in, norm_gain, query_gain, key_norm_gain, w_query, key_weight, w_value, w_out, key_cache, value_cache, lengths):
    group_size = HEADS // KEY_VALUE_HEADS
    hidden = decode_in.astype(jnp.float32) + path_embed.astype(jnp.float32)[:, None, :]
    normed = normalize(hidden, norm_gain).astype(jnp.bfloat16).reshape(PATHS * STEPS, D)
    positions = (lengths[:, None] + jnp.arange(STEPS).astype(jnp.int32)[None, :]).reshape(-1)
    dquery = project_rows(normed, w_query, query_gain, positions).reshape(PATHS, STEPS, KEY_VALUE_HEADS, group_size, HEAD_SIZE)
    dkey = project_rows(normed, key_weight, key_norm_gain, positions).reshape(PATHS, STEPS, KEY_VALUE_HEADS, HEAD_SIZE)
    dvalue = jnp.dot(normed, w_value, preferred_element_type=jnp.float32).astype(jnp.bfloat16).reshape(PATHS, STEPS, KEY_VALUE_HEADS, HEAD_SIZE)
    cache_keys = key_cache.reshape(PATHS, CACHE, KEY_VALUE_HEADS, HEAD_SIZE)
    cache_values = value_cache.reshape(PATHS, CACHE, KEY_VALUE_HEADS, HEAD_SIZE)
    slots = jnp.arange(CACHE + STEPS).astype(jnp.int32)
    step_index = jnp.arange(STEPS).astype(jnp.int32)
    per_head = jax.vmap(attend, in_axes=(1, 1, 1, None), out_axes=1)

    def one_path(inputs):
        query, ckeys, cvalues, nkeys, nvalues, length = inputs
        key_rows = jnp.concatenate([ckeys, nkeys], axis=0)
        value_rows = jnp.concatenate([cvalues, nvalues], axis=0)
        allowed = jnp.where(slots[None, :] < CACHE, slots[None, :] < length, slots[None, :] - CACHE <= step_index[:, None])
        return per_head(query, key_rows, value_rows, allowed)
    dattn = lax.map(one_path, (dquery, cache_keys, cache_values, dkey, dvalue, lengths))
    dattn = dattn.astype(jnp.bfloat16).reshape(PATHS * STEPS, HEADS * HEAD_SIZE)
    decode_out = jnp.dot(dattn, w_out, preferred_element_type=jnp.float32).astype(jnp.bfloat16).reshape(PATHS, STEPS, D)
    summary_rows_normed = normalize(summary_in.astype(jnp.float32), norm_gain).astype(jnp.bfloat16)
    summary_positions = CACHE + jnp.arange(SUMMARY_TOKENS).astype(jnp.int32)
    squery = project_rows(summary_rows_normed, w_query, query_gain, summary_positions).reshape(SUMMARY_TOKENS, KEY_VALUE_HEADS, group_size, HEAD_SIZE)
    summary_key_rows = project_rows(summary_rows_normed, key_weight, key_norm_gain, summary_positions).reshape(SUMMARY_TOKENS, KEY_VALUE_HEADS, HEAD_SIZE)
    svalue = jnp.dot(summary_rows_normed, w_value, preferred_element_type=jnp.float32).astype(jnp.bfloat16).reshape(SUMMARY_TOKENS, KEY_VALUE_HEADS, HEAD_SIZE)
    every_path_keys = jnp.concatenate([cache_keys, dkey], axis=1).reshape(PATHS * (CACHE + STEPS), KEY_VALUE_HEADS, HEAD_SIZE)
    every_path_keys = jnp.concatenate([every_path_keys, summary_key_rows], axis=0)
    all_values = jnp.concatenate([cache_values, dvalue], axis=1).reshape(PATHS * (CACHE + STEPS), KEY_VALUE_HEADS, HEAD_SIZE)
    all_values = jnp.concatenate([all_values, svalue], axis=0)
    live_slots = (slots[None, :] < lengths[:, None]) | (slots[None, :] >= CACHE)
    row_index = jnp.arange(SUMMARY_TOKENS).astype(jnp.int32)
    allowed = jnp.concatenate([jnp.broadcast_to(live_slots.reshape(1, -1), (SUMMARY_TOKENS, PATHS * (CACHE + STEPS))), row_index[None, :] <= row_index[:, None]], axis=1)

    def one_head(inputs):
        return attend(inputs[0], inputs[1], inputs[2], allowed)
    sattn = lax.map(one_head, (jnp.transpose(squery, (1, 0, 2, 3)), jnp.transpose(every_path_keys, (1, 0, 2)), jnp.transpose(all_values, (1, 0, 2))))
    sattn = jnp.transpose(sattn, (1, 0, 2, 3)).astype(jnp.bfloat16).reshape(SUMMARY_TOKENS, HEADS * HEAD_SIZE)
    summary_out = jnp.dot(sattn, w_out, preferred_element_type=jnp.float32).astype(jnp.bfloat16)
    return (decode_out, summary_out)
```

```python
import functools
import math

import jax
import jax.numpy as jnp
from jax import lax
from jax.experimental import pallas as pl
from jax.experimental.pallas import tpu as pltpu
from jax.sharding import PartitionSpec as P

EPS = 1e-06
ROPE_BASE = 1000000.0
HEAD = 128
GROUP = 4
STEPS = 4
SCALE2 = math.log2(math.e) / math.sqrt(HEAD)
NEG = -1e30
F32 = jnp.float32
BF16 = jnp.bfloat16
MIB = 1024 * 1024


def dot(a, b):
    return lax.dot_general(a, b, (((1,), (0,)), ((), ())), preferred_element_type=F32)


def dot_t(a, b):
    return lax.dot_general(a, b, (((1,), (1,)), ((), ())), preferred_element_type=F32)


def rms(rows, gain):
    factor = lax.rsqrt(jnp.mean(rows * rows, axis=-1, keepdims=True) + EPS)
    return rows * factor * gain


def rope_tables(positions):
    lane = lax.broadcasted_iota(jnp.int32, positions.shape, 1)
    exponent = (lane % (HEAD // 2)).astype(F32) * (2.0 / HEAD)
    angles = positions * jnp.exp(-math.log(ROPE_BASE) * exponent)
    sine = jnp.sin(angles)
    return jnp.cos(angles), jnp.where(lane < HEAD // 2, -sine, sine)


def rotate(v, cosine, sine):
    return v * cosine + pltpu.roll(v, HEAD // 2, 1) * sine


def decode_kernel(
    lengths, decode_in, embed, norm_gain, query_gain, key_gain, w_query, w_key, w_value, w_out,
    keys, values, dterms, dkey, dvalue, cos_out, sin_out,
):
    path = lax.axis_index("path")
    len0 = lengths[path * 2]
    len1 = lengths[path * 2 + 1]
    hidden = jnp.concatenate(
        [decode_in[i].astype(F32) + embed[i : i + 1, :].astype(F32) for i in range(2)], axis=0
    )
    normed = rms(hidden, norm_gain[...].astype(F32)).astype(BF16)
    row = lax.broadcasted_iota(jnp.int32, (8, HEAD), 0)
    position = jnp.where(row < STEPS, len0 + row, len1 + row - STEPS).astype(F32)
    cosine, sine = rope_tables(position)
    query = dot(normed, w_query[...])
    qgain = query_gain[...].astype(F32)
    heads = [
        rotate(rms(query[:, h * HEAD : (h + 1) * HEAD], qgain), cosine, sine)
        for h in range(GROUP)
    ]
    new_key = rotate(rms(dot(normed, w_key[...]), key_gain[...].astype(F32)), cosine, sine)
    new_key = new_key.astype(BF16)
    new_value = dot(normed, w_value[...]).astype(BF16)
    dkey[...] = new_key.astype(F32)
    dvalue[...] = new_value.astype(F32)
    mixed = []
    for i, length in enumerate((len0, len1)):
        q = jnp.concatenate([x[i * STEPS : (i + 1) * STEPS] for x in heads], axis=0).astype(BF16)
        cached = dot_t(q, keys[i])
        slot = lax.broadcasted_iota(jnp.int32, cached.shape, 1)
        cached = jnp.where(slot < length, cached, NEG)
        recent = dot_t(q, new_key)
        r_row = lax.broadcasted_iota(jnp.int32, recent.shape, 0) % STEPS
        r_col = lax.broadcasted_iota(jnp.int32, recent.shape, 1) - i * STEPS
        recent = jnp.where((r_col >= 0) & (r_col <= r_row), recent, NEG)
        peak = jnp.maximum(
            jnp.max(cached, axis=-1, keepdims=True), jnp.max(recent, axis=-1, keepdims=True)
        )
        wc = jnp.exp2((cached - peak) * SCALE2)
        wr = jnp.exp2((recent - peak) * SCALE2)
        total = jnp.sum(wc, axis=-1, keepdims=True) + jnp.sum(wr, axis=-1, keepdims=True)
        mix = dot(wc.astype(BF16), values[i]) + dot(wr.astype(BF16), new_value)
        mix = mix / total
        mixed.append(
            jnp.concatenate([mix[h * STEPS : (h + 1) * STEPS] for h in range(GROUP)], axis=1)
        )
    attn = jnp.concatenate(mixed, axis=0).astype(BF16)
    width = dterms.shape[2]
    for t in range(dterms.shape[0]):
        dterms[t] = dot(attn, w_out[:, t * width : (t + 1) * width]).astype(BF16)
    rows = cos_out.shape[0]
    row = lax.broadcasted_iota(jnp.int32, (rows, HEAD), 0)
    cosine, sine = rope_tables((keys.shape[1] + path * rows + row).astype(F32))
    cos_out[...] = cosine
    sin_out[...] = sine


def project_kernel(*refs):
    rows_in = refs[:8]
    (
        norm_gain, query_gain, key_gain, w_query, w_key, w_value, cosine, sine, dkey, dvalue,
        query_out, tail_keys, tail_values, normed_f32,
    ) = refs[8:]
    own = lax.axis_index("tensor")
    gain = norm_gain[...].astype(F32)
    for j in range(8):
        at = pl.multiple_of((own ^ j) * 8, 8)
        normed_f32[pl.ds(at, 8), :] = rms(rows_in[j][...].astype(F32), gain)
    normed = normed_f32[...].astype(BF16)
    cos = cosine[...]
    sin = sine[...]
    query = dot(normed, w_query[...])
    qgain = query_gain[...].astype(F32)
    for h in range(GROUP):
        at = slice(h * HEAD, (h + 1) * HEAD)
        query_out[:, at] = rotate(rms(query[:, at], qgain), cos, sin).astype(BF16)
    key = rotate(rms(dot(normed, w_key[...]), key_gain[...].astype(F32)), cos, sin)
    value = dot(normed, w_value[...])
    pad = jnp.zeros((56, HEAD), F32)
    tail_keys[...] = jnp.concatenate([key, dkey[...], pad], axis=0).astype(BF16)
    tail_values[...] = jnp.concatenate([value, dvalue[...], pad], axis=0).astype(BF16)


def attend_kernel(flip, lengths, query, keys, values, tail_keys, tail_values, out):
    path = lax.axis_index("path")
    block = path ^ flip
    rows = query.shape[0]
    q = jnp.concatenate(
        [query[:, h * HEAD : (h + 1) * HEAD] for h in range(GROUP)], axis=0
    )
    total_rows = rows * GROUP
    scores = []
    for i in range(2):
        s = dot_t(q, keys[i])
        slot = lax.broadcasted_iota(jnp.int32, s.shape, 1)
        scores.append(jnp.where(slot < lengths[path * 2 + i], s, NEG))
    s = dot_t(q, tail_keys[...])
    col = lax.broadcasted_iota(jnp.int32, s.shape, 1)
    row = lax.broadcasted_iota(jnp.int32, s.shape, 0) % rows
    causal = (col < rows) & (path * rows + col <= block * rows + row)
    recent = (col >= rows) & (col < rows + 8)
    scores.append(jnp.where(causal | recent, s, NEG))
    peak = scores[0].max(axis=-1, keepdims=True)
    for s in scores[1:]:
        peak = jnp.maximum(peak, s.max(axis=-1, keepdims=True))
    peak = (peak * SCALE2).astype(BF16).astype(F32)
    total = jnp.zeros((total_rows, 1), F32)
    mix = jnp.zeros((total_rows, HEAD), F32)
    for s, v in zip(scores, (values[0], values[1], tail_values[...])):
        w = jnp.exp2(s * SCALE2 - peak)
        total = total + jnp.sum(w, axis=-1, keepdims=True)
        mix = mix + dot(w.astype(BF16), v)
    high = total.astype(BF16).astype(F32)
    low = total - high
    lane = lax.broadcasted_iota(jnp.int32, (rows, HEAD), 1)
    stats = jnp.zeros((rows, HEAD), F32)
    for h in range(GROUP):
        at = slice(h * rows, (h + 1) * rows)
        out[:, h * HEAD : (h + 1) * HEAD] = mix[at].astype(BF16)
        for n, x in enumerate((peak, high, low)):
            stats = jnp.where(lane == n * GROUP + h, x[at], stats)
    out[:, GROUP * HEAD :] = stats.astype(BF16)


def output_kernel(own_part, part1, part2, part3, w_out, dterms, send, keep, attn):
    core = lax.axis_index("tensor") % 2
    parts = (own_part, part1, part2, part3)
    stats = [x[:, GROUP * HEAD :].astype(F32) for x in parts]
    for h in range(GROUP):
        at = slice(h * HEAD, (h + 1) * HEAD)
        peaks = [s[:, h : h + 1] for s in stats]
        peak = functools.reduce(jnp.maximum, peaks)
        mix = 0.0
        total = 0.0
        for s, p, x in zip(stats, peaks, parts):
            w = jnp.exp2(p - peak)
            total = total + w * (s[:, GROUP + h : GROUP + h + 1] + s[:, 2 * GROUP + h : 2 * GROUP + h + 1])
            mix = mix + w * x[:, at].astype(F32)
        attn[:, at] = mix / total
    width = w_out.shape[1]
    for which, ref in ((1 - core, send), (core, keep)):
        lhs = jnp.concatenate(
            [attn[pl.ds(pl.multiple_of((2 * y + which) * 8, 8), 8), :] for y in range(4)], axis=0
        ).astype(BF16)
        res = dot(lhs, w_out[...])
        for y in range(4):
            ref[y, :, :width] = res[y * 8 : (y + 1) * 8].astype(ref.dtype)
            ref[y, :, width:] = dterms[2 * y + which].astype(ref.dtype)


def fold_kernel(keep, received, own_out, out1, out2, out3):
    at = lax.axis_index("tensor") // 2
    for k, ref in enumerate((own_out, out1, out2, out3)):
        block = at ^ k
        ref[...] = (keep[block] + received[block].astype(F32)).astype(ref.dtype)


def final_kernel(own, in1, in2, in3, decode_out, summary_out):
    total = own[...] + in1[...].astype(F32) + in2[...].astype(F32) + in3[...].astype(F32)
    width = summary_out.shape[1]
    summary_out[...] = total[:, :width].astype(BF16)
    decode_out[0] = total[:STEPS, width:].astype(BF16)
    decode_out[1] = total[STEPS:, width:].astype(BF16)


def call(kernel, out_shape, args, scratch=(), limit=32, flops=0, smem=()):
    specs = [
        pl.BlockSpec(memory_space=pltpu.SMEM if i in smem else pltpu.VMEM)
        for i in range(len(args))
    ]
    nbytes = sum(math.prod(a.shape) * a.dtype.itemsize for a in args)
    outs = tuple(jax.ShapeDtypeStruct(s, d) for s, d in out_shape)
    out = pl.pallas_call(
        kernel,
        out_shape=outs,
        in_specs=specs,
        out_specs=tuple(pl.BlockSpec(memory_space=pltpu.VMEM) for _ in outs),
        scratch_shapes=list(scratch),
        compiler_params=pltpu.CompilerParams(vmem_limit_bytes=limit * MIB),
        cost_estimate=pl.CostEstimate(flops=flops, bytes_accessed=nbytes, transcendentals=0),
    )(*args)
    return out


def flip(x, axis, size, k):
    return lax.ppermute(x, axis, [(i, i ^ k) for i in range(size)])


def body(
    decode_in,
    path_embed,
    summary_in,
    norm_gain,
    query_gain,
    key_norm_gain,
    w_query,
    key_weight,
    w_value,
    w_out,
    key_cache,
    value_cache,
    lengths,
):
    width = w_out.shape[1]
    rows = 64
    norm_gain = norm_gain.reshape(1, -1)
    query_gain = query_gain.reshape(1, -1)
    key_gain = key_norm_gain.reshape(1, -1)

    across = {k: flip(summary_in, "tensor", 8, k) for k in (2, 6, 4)}
    across[0] = summary_in
    row_blocks = [None] * 8
    for k in (0, 2, 6, 4):
        row_blocks[k] = across[k]
        row_blocks[k + 1] = flip(across[k], "tensor", 8, 1)

    dterms, dkey, dvalue, cosine, sine = call(
        decode_kernel,
        [((8, 8, width // 8), BF16), ((8, HEAD), F32), ((8, HEAD), F32), ((rows, HEAD), F32), ((rows, HEAD), F32)],
        (lengths, decode_in, path_embed, norm_gain, query_gain, key_gain, w_query, key_weight,
         w_value, w_out, key_cache, value_cache),
        limit=24,
        smem=(0,),
        flops=2 * 8 * 4096 * 5000,
    )

    query, tail_keys, tail_values = call(
        project_kernel,
        [((rows, GROUP * HEAD), BF16), ((128, HEAD), BF16), ((128, HEAD), BF16)],
        (*row_blocks, norm_gain, query_gain, key_gain, w_query, key_weight, w_value, cosine, sine,
         dkey, dvalue),
        scratch=[pltpu.VMEM((rows, width), F32)],
        limit=24,
        flops=2 * 64 * 4096 * 768,
    )

    queries = [query] + [flip(query, "path", 4, k) for k in (1, 2, 3)]
    parts = []
    for k in range(4):
        (part,) = call(
            functools.partial(attend_kernel, k),
            [((rows, (GROUP + 1) * HEAD), BF16)],
            (lengths, queries[k], key_cache, value_cache, tail_keys, tail_values),
            limit=32,
            smem=(0,),
            flops=4 * 256 * 4224 * 128,
        )
        parts.append(part if k == 0 else flip(part, "path", 4, k))

    send, keep = call(
        output_kernel,
        [((4, 8, width + width // 8), BF16), ((4, 8, width + width // 8), F32)],
        (*parts, w_out, dterms),
        scratch=[pltpu.VMEM((rows, GROUP * HEAD), F32)],
        limit=24,
        flops=2 * 64 * 512 * 4096,
    )
    received = flip(send, "tensor", 8, 1)
    own, out1, out2, out3 = call(
        fold_kernel,
        [((8, width + width // 8), F32)] + [((8, width + width // 8), BF16)] * 3,
        (keep, received),
    )
    in1 = flip(out1, "tensor", 8, 2)
    in2 = flip(out2, "tensor", 8, 4)
    in3 = flip(out3, "tensor", 8, 6)
    decode_out, summary_out = call(
        final_kernel,
        [((2, STEPS, width // 8), BF16), ((8, width), BF16)],
        (own, in1, in2, in3),
    )
    return (decode_out, summary_out)


def solution(mesh):
    in_specs = (
        P(("problem", "path"), None, None),
        P("path", None),
        P(("problem", "path", "tensor"), None),
        P(),
        P(),
        P(),
        P(None, "tensor"),
        P(None, "tensor"),
        P(None, "tensor"),
        P("tensor", None),
        P(("problem", "path"), None, "tensor"),
        P(("problem", "path"), None, "tensor"),
        P("problem"),
    )
    out_specs = (P(("problem", "path"), None, "tensor"), P(("problem", "path", "tensor"), None))
    return jax.shard_map(body, mesh=mesh, in_specs=in_specs, out_specs=out_specs, check_vma=False)
```

```python
import functools
import math

import jax
import jax.numpy as jnp
from jax import lax
from jax.experimental import pallas as pl
from jax.experimental.pallas import tpu as pltpu
from jax.sharding import PartitionSpec as P

EPS = 1e-06
ROPE_BASE = 1000000.0
HEAD = 128
GROUP = 4
STEPS = 4
SCALE2 = math.log2(math.e) / math.sqrt(HEAD)
NEG = -1e30
F32 = jnp.float32
BF16 = jnp.bfloat16
MIB = 1024 * 1024


def dot(a, b):
    return lax.dot_general(a, b, (((1,), (0,)), ((), ())), preferred_element_type=F32)


def dot_t(a, b):
    return lax.dot_general(a, b, (((1,), (1,)), ((), ())), preferred_element_type=F32)


def rms(rows, gain):
    factor = lax.rsqrt(jnp.mean(rows * rows, axis=-1, keepdims=True) + EPS)
    return rows * factor * gain


def rope_tables(positions):
    lane = lax.broadcasted_iota(jnp.int32, positions.shape, 1)
    exponent = (lane % (HEAD // 2)).astype(F32) * (2.0 / HEAD)
    angles = positions * jnp.exp(-math.log(ROPE_BASE) * exponent)
    sine = jnp.sin(angles)
    return jnp.cos(angles), jnp.where(lane < HEAD // 2, -sine, sine)


def rotate(v, cosine, sine):
    return v * cosine + pltpu.roll(v, HEAD // 2, 1) * sine


def decode_kernel(
    lengths, decode_in, embed, norm_gain, query_gain, key_gain, w_query, w_key, w_value, w_out,
    keys, values, dterms, dkey, dvalue, cos_out, sin_out,
):
    path = lax.axis_index("path")
    len0 = lengths[path * 2]
    len1 = lengths[path * 2 + 1]
    hidden = jnp.concatenate(
        [decode_in[i].astype(F32) + embed[i : i + 1, :].astype(F32) for i in range(2)], axis=0
    )
    normed = rms(hidden, norm_gain[...].astype(F32)).astype(BF16)
    row = lax.broadcasted_iota(jnp.int32, (8, HEAD), 0)
    position = jnp.where(row < STEPS, len0 + row, len1 + row - STEPS).astype(F32)
    cosine, sine = rope_tables(position)
    rows = cos_out.shape[0]
    row = lax.broadcasted_iota(jnp.int32, (rows, HEAD), 0)
    cos_all, sin_all = rope_tables((keys.shape[1] + path * rows + row).astype(F32))
    cos_out[...] = cos_all
    sin_out[...] = sin_all
    query = dot(normed, w_query[...])
    qgain = query_gain[...].astype(F32)
    heads = [
        rotate(rms(query[:, h * HEAD : (h + 1) * HEAD], qgain), cosine, sine)
        for h in range(GROUP)
    ]
    new_key = rotate(rms(dot(normed, w_key[...]), key_gain[...].astype(F32)), cosine, sine)
    new_key = new_key.astype(BF16)
    new_value = dot(normed, w_value[...]).astype(BF16)
    dkey[...] = new_key.astype(F32)
    dvalue[...] = new_value.astype(F32)
    mixed = []
    for i, length in enumerate((len0, len1)):
        q = jnp.concatenate([x[i * STEPS : (i + 1) * STEPS] for x in heads], axis=0).astype(BF16)
        cached = dot_t(q, keys[i])
        slot = lax.broadcasted_iota(jnp.int32, cached.shape, 1)
        cached = jnp.where(slot < length, cached, NEG)
        recent = dot_t(q, new_key)
        r_row = lax.broadcasted_iota(jnp.int32, recent.shape, 0) % STEPS
        r_col = lax.broadcasted_iota(jnp.int32, recent.shape, 1) - i * STEPS
        recent = jnp.where((r_col >= 0) & (r_col <= r_row), recent, NEG)
        peak = jnp.maximum(
            jnp.max(cached, axis=-1, keepdims=True), jnp.max(recent, axis=-1, keepdims=True)
        )
        wc = jnp.exp2((cached - peak) * SCALE2)
        wr = jnp.exp2((recent - peak) * SCALE2)
        total = jnp.sum(wc, axis=-1, keepdims=True) + jnp.sum(wr, axis=-1, keepdims=True)
        mix = dot(wc.astype(BF16), values[i]) + dot(wr.astype(BF16), new_value)
        mix = mix / total
        mixed.append(
            jnp.concatenate([mix[h * STEPS : (h + 1) * STEPS] for h in range(GROUP)], axis=1)
        )
    attn = jnp.concatenate(mixed, axis=0).astype(BF16)
    width = dterms.shape[2]
    for t in range(dterms.shape[0]):
        dterms[t] = dot(attn, w_out[:, t * width : (t + 1) * width]).astype(BF16)


def hold_kernel(rows, out):
    out[...] = rows[...]


def norm_kernel(rows0, rows1, rows2, rows3, gain, dkey, dvalue, out, tail_key, tail_value):
    for k, ref in enumerate((rows0, rows1, rows2, rows3)):
        out[k] = rms(ref[...].astype(F32), gain[...].astype(F32)).astype(BF16)
    tail_key[...] = dkey[...]
    tail_value[...] = dvalue[...]


def project_kernel(
    mine, other, query_gain, key_gain, w_query, w_key, w_value, cosine, sine, dkey, dvalue,
    query_out, tail_keys, tail_values, normed_f32,
):
    own = lax.axis_index("tensor")
    for k in range(4):
        for flipped, ref in ((0, mine), (1, other)):
            at = pl.multiple_of((own ^ (2 * k + flipped)) * 8, 8)
            normed_f32[pl.ds(at, 8), :] = ref[k].astype(F32)
    normed = normed_f32[...].astype(BF16)
    cos = cosine[...]
    sin = sine[...]
    query = dot(normed, w_query[...])
    qgain = query_gain[...].astype(F32)
    for h in range(GROUP):
        at = slice(h * HEAD, (h + 1) * HEAD)
        query_out[:, at] = rotate(rms(query[:, at], qgain), cos, sin).astype(BF16)
    key = rotate(rms(dot(normed, w_key[...]), key_gain[...].astype(F32)), cos, sin)
    value = dot(normed, w_value[...])
    pad = jnp.zeros((56, HEAD), F32)
    tail_keys[...] = jnp.concatenate([key, dkey[...], pad], axis=0).astype(BF16)
    tail_values[...] = jnp.concatenate([value, dvalue[...], pad], axis=0).astype(BF16)


def attend_kernel(flip, lengths, query, keys, values, tail_keys, tail_values, out):
    path = lax.axis_index("path")
    block = path ^ flip
    rows = query.shape[0]
    q = jnp.concatenate(
        [query[:, h * HEAD : (h + 1) * HEAD] for h in range(GROUP)], axis=0
    )
    total_rows = rows * GROUP
    scores = []
    for i in range(2):
        s = dot_t(q, keys[i])
        slot = lax.broadcasted_iota(jnp.int32, s.shape, 1)
        scores.append(jnp.where(slot < lengths[path * 2 + i], s, NEG))
    s = dot_t(q, tail_keys[...])
    col = lax.broadcasted_iota(jnp.int32, s.shape, 1)
    row = lax.broadcasted_iota(jnp.int32, s.shape, 0) % rows
    causal = (col < rows) & (path * rows + col <= block * rows + row)
    recent = (col >= rows) & (col < rows + 8)
    scores.append(jnp.where(causal | recent, s, NEG))
    peak = scores[0].max(axis=-1, keepdims=True)
    for s in scores[1:]:
        peak = jnp.maximum(peak, s.max(axis=-1, keepdims=True))
    peak = (peak * SCALE2).astype(BF16).astype(F32)
    total = jnp.zeros((total_rows, 1), F32)
    mix = jnp.zeros((total_rows, HEAD), F32)
    for s, v in zip(scores, (values[0], values[1], tail_values[...])):
        w = jnp.exp2(s * SCALE2 - peak)
        total = total + jnp.sum(w, axis=-1, keepdims=True)
        mix = mix + dot(w.astype(BF16), v)
    high = total.astype(BF16).astype(F32)
    low = total - high
    lane = lax.broadcasted_iota(jnp.int32, (rows, HEAD), 1)
    stats = jnp.zeros((rows, HEAD), F32)
    for h in range(GROUP):
        at = slice(h * rows, (h + 1) * rows)
        out[:, h * HEAD : (h + 1) * HEAD] = mix[at].astype(BF16)
        for n, x in enumerate((peak, high, low)):
            stats = jnp.where(lane == n * GROUP + h, x[at], stats)
    out[:, GROUP * HEAD :] = stats.astype(BF16)


def output_kernel(own_part, part1, part2, part3, w_out, dterms, send, keep, attn):
    core = lax.axis_index("tensor") % 2
    parts = (own_part, part1, part2, part3)
    stats = [x[:, GROUP * HEAD :].astype(F32) for x in parts]
    for h in range(GROUP):
        at = slice(h * HEAD, (h + 1) * HEAD)
        peaks = [s[:, h : h + 1] for s in stats]
        peak = functools.reduce(jnp.maximum, peaks)
        mix = 0.0
        total = 0.0
        for s, p, x in zip(stats, peaks, parts):
            w = jnp.exp2(p - peak)
            total = total + w * (s[:, GROUP + h : GROUP + h + 1] + s[:, 2 * GROUP + h : 2 * GROUP + h + 1])
            mix = mix + w * x[:, at].astype(F32)
        attn[:, at] = mix / total
    width = w_out.shape[1]
    for which, ref in ((1 - core, send), (core, keep)):
        lhs = jnp.concatenate(
            [attn[pl.ds(pl.multiple_of((2 * y + which) * 8, 8), 8), :] for y in range(4)], axis=0
        ).astype(BF16)
        res = dot(lhs, w_out[...])
        for y in range(4):
            ref[y, :, :width] = res[y * 8 : (y + 1) * 8].astype(ref.dtype)
            ref[y, :, width:] = dterms[2 * y + which].astype(ref.dtype)


def fold_kernel(keep, received, own_out, out1, out2, out3):
    at = lax.axis_index("tensor") // 2
    for k, ref in enumerate((own_out, out1, out2, out3)):
        block = at ^ k
        ref[...] = (keep[block] + received[block].astype(F32)).astype(ref.dtype)


def final_kernel(own, in1, in2, in3, decode_out, summary_out):
    total = own[...] + in1[...].astype(F32) + in2[...].astype(F32) + in3[...].astype(F32)
    width = summary_out.shape[1]
    summary_out[...] = total[:, :width].astype(BF16)
    decode_out[0] = total[:STEPS, width:].astype(BF16)
    decode_out[1] = total[STEPS:, width:].astype(BF16)


def call(kernel, out_shape, args, scratch=(), limit=32, flops=0, smem=(), far=(), nbytes=None):
    specs = [
        pl.BlockSpec(
            memory_space=pltpu.SMEM if i in smem else pltpu.HBM if i in far else pltpu.VMEM
        )
        for i in range(len(args))
    ]
    if nbytes is None:
        nbytes = sum(math.prod(a.shape) * a.dtype.itemsize for a in args)
    outs = tuple(jax.ShapeDtypeStruct(s, d) for s, d in out_shape)
    out = pl.pallas_call(
        kernel,
        out_shape=outs,
        in_specs=specs,
        out_specs=tuple(pl.BlockSpec(memory_space=pltpu.VMEM) for _ in outs),
        scratch_shapes=list(scratch),
        compiler_params=pltpu.CompilerParams(vmem_limit_bytes=limit * MIB),
        cost_estimate=pl.CostEstimate(flops=flops, bytes_accessed=nbytes, transcendentals=0),
    )(*args)
    return out


def flip(x, axis, size, k):
    return lax.ppermute(x, axis, [(i, i ^ k) for i in range(size)])


def body(
    decode_in,
    path_embed,
    summary_in,
    norm_gain,
    query_gain,
    key_norm_gain,
    w_query,
    key_weight,
    w_value,
    w_out,
    key_cache,
    value_cache,
    lengths,
):
    width = w_out.shape[1]
    rows = 64
    norm_gain = norm_gain.reshape(1, -1)
    query_gain = query_gain.reshape(1, -1)
    key_gain = key_norm_gain.reshape(1, -1)

    (own_rows,) = call(hold_kernel, [(summary_in.shape, BF16)], (summary_in,), flops=10**10)
    across = [own_rows] + [flip(own_rows, "tensor", 8, k) for k in (2, 4, 6)]

    dterms, dkey, dvalue, cosine, sine = call(
        decode_kernel,
        [((8, 8, width // 8), BF16), ((8, HEAD), F32), ((8, HEAD), F32), ((rows, HEAD), F32), ((rows, HEAD), F32)],
        (lengths, decode_in, path_embed, norm_gain, query_gain, key_gain, w_query, key_weight,
         w_value, w_out, key_cache, value_cache),
        limit=24,
        smem=(0,),
        flops=6 * 10**9,
    )

    mine, dkey, dvalue = call(
        norm_kernel,
        [((4, 8, width), BF16), ((8, HEAD), F32), ((8, HEAD), F32)],
        (*across, norm_gain, dkey, dvalue),
    )
    other = flip(mine, "tensor", 8, 1)
    query, tail_keys, tail_values = call(
        project_kernel,
        [((rows, GROUP * HEAD), BF16), ((128, HEAD), BF16), ((128, HEAD), BF16)],
        (mine, other, query_gain, key_gain, w_query, key_weight, w_value, cosine, sine,
         dkey, dvalue),
        scratch=[pltpu.VMEM((rows, width), F32)],
        limit=24,
        flops=2 * 64 * 4096 * 768,
    )

    queries = [query] + [flip(query, "path", 4, k) for k in (1, 2, 3)]
    parts = []
    for k in range(4):
        (part,) = call(
            functools.partial(attend_kernel, k),
            [((rows, (GROUP + 1) * HEAD), BF16)],
            (lengths, queries[k], key_cache, value_cache, tail_keys, tail_values),
            limit=32,
            smem=(0,),
            flops=4 * 256 * 4224 * 128,
        )
        parts.append(part if k == 0 else flip(part, "path", 4, k))

    send, keep = call(
        output_kernel,
        [((4, 8, width + width // 8), BF16), ((4, 8, width + width // 8), F32)],
        (*parts, w_out, dterms),
        scratch=[pltpu.VMEM((rows, GROUP * HEAD), F32)],
        limit=24,
        flops=2 * 64 * 512 * 4096,
    )
    received = flip(send, "tensor", 8, 1)
    own, out1, out2, out3 = call(
        fold_kernel,
        [((8, width + width // 8), F32)] + [((8, width + width // 8), BF16)] * 3,
        (keep, received),
    )
    in1 = flip(out1, "tensor", 8, 2)
    in2 = flip(out2, "tensor", 8, 4)
    in3 = flip(out3, "tensor", 8, 6)
    decode_out, summary_out = call(
        final_kernel,
        [((2, STEPS, width // 8), BF16), ((8, width), BF16)],
        (own, in1, in2, in3),
    )
    return (decode_out, summary_out)


def solution(mesh):
    in_specs = (
        P(("problem", "path"), None, None),
        P("path", None),
        P(("problem", "path", "tensor"), None),
        P(),
        P(),
        P(),
        P(None, "tensor"),
        P(None, "tensor"),
        P(None, "tensor"),
        P("tensor", None),
        P(("problem", "path"), None, "tensor"),
        P(("problem", "path"), None, "tensor"),
        P("problem"),
    )
    out_specs = (P(("problem", "path"), None, "tensor"), P(("problem", "path", "tensor"), None))
    return jax.shard_map(body, mesh=mesh, in_specs=in_specs, out_specs=out_specs, check_vma=False)
```

```python
import functools
import math

import jax
import jax.numpy as jnp
from jax import lax
from jax.experimental import pallas as pl
from jax.experimental.pallas import tpu as pltpu
from jax.sharding import PartitionSpec as P

EPS = 1e-06
ROPE_BASE = 1000000.0
HEAD = 128
GROUP = 4
STEPS = 4
SCALE2 = math.log2(math.e) / math.sqrt(HEAD)
NEG = -1e30
CHUNK = 1024
F32 = jnp.float32
BF16 = jnp.bfloat16
MIB = 1024 * 1024


def dot(a, b):
    return lax.dot_general(a, b, (((1,), (0,)), ((), ())), preferred_element_type=F32)


def dot_t(a, b):
    return lax.dot_general(a, b, (((1,), (1,)), ((), ())), preferred_element_type=F32)


def rms(rows, gain):
    factor = lax.rsqrt(jnp.mean(rows * rows, axis=-1, keepdims=True) + EPS)
    return rows * factor * gain


def rope_tables(positions):
    lane = lax.broadcasted_iota(jnp.int32, positions.shape, 1)
    exponent = (lane % (HEAD // 2)).astype(F32) * (2.0 / HEAD)
    angles = positions * jnp.exp(-math.log(ROPE_BASE) * exponent)
    sine = jnp.sin(angles)
    return jnp.cos(angles), jnp.where(lane < HEAD // 2, -sine, sine)


def rotate(v, cosine, sine):
    return v * cosine + pltpu.roll(v, HEAD // 2, 1) * sine


def decode_kernel(
    lengths, decode_in, embed, norm_gain, query_gain, key_gain, w_query, w_key, w_value, w_out,
    keys, values, dterms, dkey, dvalue, cos_out, sin_out,
):
    path = lax.axis_index("path")
    len0 = lengths[path * 2]
    len1 = lengths[path * 2 + 1]
    hidden = jnp.concatenate(
        [decode_in[i].astype(F32) + embed[i : i + 1, :].astype(F32) for i in range(2)], axis=0
    )
    normed = rms(hidden, norm_gain[...].astype(F32)).astype(BF16)
    row = lax.broadcasted_iota(jnp.int32, (8, HEAD), 0)
    position = jnp.where(row < STEPS, len0 + row, len1 + row - STEPS).astype(F32)
    cosine, sine = rope_tables(position)
    rows = cos_out.shape[0]
    row = lax.broadcasted_iota(jnp.int32, (rows, HEAD), 0)
    cos_all, sin_all = rope_tables((keys.shape[1] + path * rows + row).astype(F32))
    cos_out[...] = cos_all
    sin_out[...] = sin_all
    query = dot(normed, w_query[...])
    qgain = query_gain[...].astype(F32)
    heads = [
        rotate(rms(query[:, h * HEAD : (h + 1) * HEAD], qgain), cosine, sine)
        for h in range(GROUP)
    ]
    new_key = rotate(rms(dot(normed, w_key[...]), key_gain[...].astype(F32)), cosine, sine)
    new_key = new_key.astype(BF16)
    new_value = dot(normed, w_value[...]).astype(BF16)
    dkey[...] = new_key.astype(F32)
    dvalue[...] = new_value.astype(F32)
    mixed = []
    for i, length in enumerate((len0, len1)):
        q = jnp.concatenate([x[i * STEPS : (i + 1) * STEPS] for x in heads], axis=0).astype(BF16)
        cached = dot_t(q, keys[i])
        slot = lax.broadcasted_iota(jnp.int32, cached.shape, 1)
        cached = jnp.where(slot < length, cached, NEG)
        recent = dot_t(q, new_key)
        r_row = lax.broadcasted_iota(jnp.int32, recent.shape, 0) % STEPS
        r_col = lax.broadcasted_iota(jnp.int32, recent.shape, 1) - i * STEPS
        recent = jnp.where((r_col >= 0) & (r_col <= r_row), recent, NEG)
        peak = jnp.maximum(
            jnp.max(cached, axis=-1, keepdims=True), jnp.max(recent, axis=-1, keepdims=True)
        )
        wc = jnp.exp2((cached - peak) * SCALE2)
        wr = jnp.exp2((recent - peak) * SCALE2)
        total = jnp.sum(wc, axis=-1, keepdims=True) + jnp.sum(wr, axis=-1, keepdims=True)
        mix = dot(wc.astype(BF16), values[i]) + dot(wr.astype(BF16), new_value)
        mix = mix / total
        mixed.append(
            jnp.concatenate([mix[h * STEPS : (h + 1) * STEPS] for h in range(GROUP)], axis=1)
        )
    attn = jnp.concatenate(mixed, axis=0).astype(BF16)
    width = dterms.shape[2]
    for t in range(dterms.shape[0]):
        dterms[t] = dot(attn, w_out[:, t * width : (t + 1) * width]).astype(BF16)


def hold_kernel(rows, out):
    out[...] = rows[...]


def norm_kernel(rows0, rows1, rows2, rows3, gain, dkey, dvalue, out, tail_key, tail_value):
    for k, ref in enumerate((rows0, rows1, rows2, rows3)):
        out[k] = rms(ref[...].astype(F32), gain[...].astype(F32)).astype(BF16)
    tail_key[...] = dkey[...]
    tail_value[...] = dvalue[...]


def project_kernel(
    mine, other, query_gain, key_gain, w_query, w_key, w_value, cosine, sine, dkey, dvalue,
    query_out, tail_keys, tail_values, normed_f32,
):
    own = lax.axis_index("tensor")
    for k in range(4):
        for flipped, ref in ((0, mine), (1, other)):
            at = pl.multiple_of((own ^ (2 * k + flipped)) * 8, 8)
            normed_f32[pl.ds(at, 8), :] = ref[k].astype(F32)
    normed = normed_f32[...].astype(BF16)
    cos = cosine[...]
    sin = sine[...]
    query = dot(normed, w_query[...])
    qgain = query_gain[...].astype(F32)
    for h in range(GROUP):
        at = slice(h * HEAD, (h + 1) * HEAD)
        query_out[:, at] = rotate(rms(query[:, at], qgain), cos, sin).astype(BF16)
    key = rotate(rms(dot(normed, w_key[...]), key_gain[...].astype(F32)), cos, sin)
    value = dot(normed, w_value[...])
    pad = jnp.zeros((56, HEAD), F32)
    tail_keys[...] = jnp.concatenate([key, dkey[...], pad], axis=0).astype(BF16)
    tail_values[...] = jnp.concatenate([value, dvalue[...], pad], axis=0).astype(BF16)


def attend_kernel(
    flip, lengths, query, keys, values, tail_keys, tail_values, _, out
):
    path = lax.axis_index("path")
    block = path ^ flip
    rows = out.shape[0]
    q = jnp.concatenate([query[:, h * HEAD : (h + 1) * HEAD] for h in range(GROUP)], axis=0)
    chunks = [(i, c) for i in range(2) for c in range(0, keys.shape[1], CHUNK)]

    def tail_scores():
        s = dot_t(q, tail_keys[...])
        col = lax.broadcasted_iota(jnp.int32, s.shape, 1)
        row = lax.broadcasted_iota(jnp.int32, s.shape, 0) % rows
        causal = (col < rows) & (path * rows + col <= block * rows + row)
        recent = (col >= rows) & (col < rows + 8)
        return jnp.where(causal | recent, s, NEG)

    def chunk_scores(i, c):
        s = dot_t(q, keys[i, c : c + CHUNK, :])
        slot = lax.broadcasted_iota(jnp.int32, (1, CHUNK), 1) + c
        return s + jnp.where(slot < lengths[path * 2 + i], 0.0, NEG)

    scores = tail_scores()
    peak = jnp.max(scores, axis=-1, keepdims=True) * SCALE2
    coming = chunk_scores(*chunks[0])
    w = jnp.exp2(scores * SCALE2 - peak)
    total = jnp.sum(w, axis=-1, keepdims=True)
    mix = dot(w.astype(BF16), tail_values[...])
    for n, (i, c) in enumerate(chunks):
        scores = coming
        if n + 1 < len(chunks):
            coming = chunk_scores(*chunks[n + 1])
        higher = jnp.maximum(peak, jnp.max(scores, axis=-1, keepdims=True) * SCALE2)
        fade = jnp.exp2(peak - higher)
        w = jnp.exp2(scores * SCALE2 - higher)
        total = total * fade + jnp.sum(w, axis=-1, keepdims=True)
        mix = mix * fade + dot(w.astype(BF16), values[i, c : c + CHUNK, :])
        peak = higher
    rounded = peak.astype(BF16).astype(F32)
    fade = jnp.exp2(peak - rounded)
    write_part(out, rows, mix * fade, rounded, total * fade)


def write_part(out, rows, mix, peak, total):
    high = total.astype(BF16).astype(F32)
    low = total - high
    lane = lax.broadcasted_iota(jnp.int32, (rows, HEAD), 1)
    stats = jnp.zeros((rows, HEAD), F32)
    for h in range(GROUP):
        at = slice(h * rows, (h + 1) * rows)
        out[:, h * HEAD : (h + 1) * HEAD] = mix[at].astype(BF16)
        for n, x in enumerate((peak, high, low)):
            stats = jnp.where(lane == n * GROUP + h, x[at], stats)
    out[:, GROUP * HEAD :] = stats.astype(BF16)


def merge(parts):
    mixes = []
    totals = []
    peak = functools.reduce(jnp.maximum, [p for _, p, _ in parts])
    scales = [jnp.exp2(p - peak) for _, p, _ in parts]
    total = sum(w * t for w, (_, _, t) in zip(scales, parts))
    for h in range(GROUP):
        at = slice(h * HEAD, (h + 1) * HEAD)
        mixes.append(sum(w[:, h : h + 1] * x[:, at] for w, (x, _, _) in zip(scales, parts)))
    return mixes, peak, total


def read_part(part):
    width = GROUP * HEAD
    stats = part[:, width:].astype(F32)
    total = stats[:, GROUP : 2 * GROUP] + stats[:, 2 * GROUP : 3 * GROUP]
    return part[:, :width].astype(F32), stats[:, :GROUP], total


def merge_kernel(part, received, out):
    rows = part.shape[0]
    mixes, peak, total = merge([read_part(part[...]), read_part(received[...])])
    mix = jnp.concatenate(mixes, axis=0)
    peak, total = (
        jnp.concatenate([x[:, h : h + 1] for h in range(GROUP)], axis=0) for x in (peak, total)
    )
    write_part(out, rows, mix, peak, total)


def project_half(attn, which, w_out, dterms, ref):
    width = w_out.shape[1]
    lhs = jnp.concatenate(
        [attn[pl.ds(pl.multiple_of((2 * y + which) * 8, 8), 8), :] for y in range(4)], axis=0
    ).astype(BF16)
    res = dot(lhs, w_out[...])
    for y in range(4):
        ref[y, :, :width] = res[y * 8 : (y + 1) * 8].astype(ref.dtype)
        ref[y, :, width:] = dterms[2 * y + which].astype(ref.dtype)


def send_kernel(own_part, part1, part2, w_out, dterms, send, attn):
    core = lax.axis_index("tensor") % 2
    parts = (own_part[...], part1[...], part2[...])
    mixes, _, total = merge([read_part(x) for x in parts])
    for h in range(GROUP):
        attn[:, h * HEAD : (h + 1) * HEAD] = mixes[h] / total[:, h : h + 1]
    project_half(attn, 1 - core, w_out, dterms, send)


def keep_kernel(attn, w_out, dterms, keep):
    project_half(attn, lax.axis_index("tensor") % 2, w_out, dterms, keep)


def fold_kernel(keep, received, own_out, out1, out2, out3):
    at = lax.axis_index("tensor") // 2
    for k, ref in enumerate((own_out, out1, out2, out3)):
        block = at ^ k
        ref[...] = (keep[block] + received[block].astype(F32)).astype(ref.dtype)


def final_kernel(own, in1, in2, in3, decode_out, summary_out):
    total = own[...] + in1[...].astype(F32) + in2[...].astype(F32) + in3[...].astype(F32)
    width = summary_out.shape[1]
    summary_out[...] = total[:, :width].astype(BF16)
    decode_out[0] = total[:STEPS, width:].astype(BF16)
    decode_out[1] = total[STEPS:, width:].astype(BF16)


def call(kernel, out_shape, args, scratch=(), limit=32, flops=0, smem=(), far=(), nbytes=None):
    specs = [
        pl.BlockSpec(
            memory_space=pltpu.SMEM if i in smem else pltpu.HBM if i in far else pltpu.VMEM
        )
        for i in range(len(args))
    ]
    if nbytes is None:
        nbytes = sum(math.prod(a.shape) * a.dtype.itemsize for a in args)
    outs = tuple(jax.ShapeDtypeStruct(s, d) for s, d in out_shape)
    out = pl.pallas_call(
        kernel,
        out_shape=outs,
        in_specs=specs,
        out_specs=tuple(pl.BlockSpec(memory_space=pltpu.VMEM) for _ in outs),
        scratch_shapes=list(scratch),
        compiler_params=pltpu.CompilerParams(vmem_limit_bytes=limit * MIB),
        cost_estimate=pl.CostEstimate(flops=flops, bytes_accessed=nbytes, transcendentals=0),
    )(*args)
    return out


def flip(x, axis, size, k):
    return lax.ppermute(x, axis, [(i, i ^ k) for i in range(size)])


def body(
    decode_in,
    path_embed,
    summary_in,
    norm_gain,
    query_gain,
    key_norm_gain,
    w_query,
    key_weight,
    w_value,
    w_out,
    key_cache,
    value_cache,
    lengths,
):
    width = w_out.shape[1]
    rows = 64
    norm_gain = norm_gain.reshape(1, -1)
    query_gain = query_gain.reshape(1, -1)
    key_gain = key_norm_gain.reshape(1, -1)

    (own_rows,) = call(hold_kernel, [(summary_in.shape, BF16)], (summary_in,), flops=10**10)
    across = [own_rows] + [flip(own_rows, "tensor", 8, k) for k in (2, 4, 6)]

    dterms, dkey, dvalue, cosine, sine = call(
        decode_kernel,
        [((8, 8, width // 8), BF16), ((8, HEAD), F32), ((8, HEAD), F32), ((rows, HEAD), F32), ((rows, HEAD), F32)],
        (lengths, decode_in, path_embed, norm_gain, query_gain, key_gain, w_query, key_weight,
         w_value, w_out, key_cache, value_cache),
        limit=24,
        smem=(0,),
        flops=6 * 10**9,
    )

    mine, dkey, dvalue = call(
        norm_kernel,
        [((4, 8, width), BF16), ((8, HEAD), F32), ((8, HEAD), F32)],
        (*across, norm_gain, dkey, dvalue),
    )
    other = flip(mine, "tensor", 8, 1)
    query, *tails = call(
        project_kernel,
        [((rows, GROUP * HEAD), BF16), ((128, HEAD), BF16), ((128, HEAD), BF16)],
        (mine, other, query_gain, key_gain, w_query, key_weight, w_value, cosine, sine, dkey, dvalue),
        scratch=[pltpu.VMEM((rows, width), F32)],
        limit=24,
        flops=2 * 64 * 4096 * 768,
    )
    queries = {0: query}
    for k in (3, 2, 1):
        queries[k] = flip(query, "path", 4, k)

    def attend(k, after):
        (part,) = call(
            functools.partial(attend_kernel, k),
            [((rows, (GROUP + 1) * HEAD), BF16)],
            (lengths, queries[k], key_cache, value_cache, *tails, after),
            limit=24,
            smem=(0,),
            flops=3 * 10**9,
        )
        return part

    part3 = attend(3, query)
    received3 = flip(part3, "path", 4, 1)
    part2 = attend(2, part3)
    (merged2,) = call(
        merge_kernel, [(part2.shape, BF16)], (part2, received3), limit=24, flops=10**8
    )
    received2 = flip(merged2, "path", 4, 2)
    part1 = attend(1, merged2)
    received1 = flip(part1, "path", 4, 1)
    own_part = attend(0, part1)
    send, attn = call(
        send_kernel,
        [((4, 8, width + width // 8), BF16), ((rows, GROUP * HEAD), F32)],
        (own_part, received1, received2, w_out, dterms),
        limit=24,
        flops=64 * 512 * 4096,
    )
    received = flip(send, "tensor", 8, 1)
    (keep,) = call(
        keep_kernel,
        [((4, 8, width + width // 8), F32)],
        (attn, w_out, dterms),
        limit=24,
        flops=64 * 512 * 4096,
    )
    own, out1, out2, out3 = call(
        fold_kernel,
        [((8, width + width // 8), F32)] + [((8, width + width // 8), BF16)] * 3,
        (keep, received),
    )
    in1 = flip(out1, "tensor", 8, 2)
    in2 = flip(out2, "tensor", 8, 4)
    in3 = flip(out3, "tensor", 8, 6)
    decode_out, summary_out = call(
        final_kernel,
        [((2, STEPS, width // 8), BF16), ((8, width), BF16)],
        (own, in1, in2, in3),
    )
    return (decode_out, summary_out)


def solution(mesh):
    in_specs = (
        P(("problem", "path"), None, None),
        P("path", None),
        P(("problem", "path", "tensor"), None),
        P(),
        P(),
        P(),
        P(None, "tensor"),
        P(None, "tensor"),
        P(None, "tensor"),
        P("tensor", None),
        P(("problem", "path"), None, "tensor"),
        P(("problem", "path"), None, "tensor"),
        P("problem"),
    )
    out_specs = (P(("problem", "path"), None, "tensor"), P(("problem", "path", "tensor"), None))
    return jax.shard_map(body, mesh=mesh, in_specs=in_specs, out_specs=out_specs, check_vma=False)
```

```python
import functools
import math

import jax
import jax.numpy as jnp
from jax import lax
from jax.experimental import pallas as pl
from jax.experimental.pallas import tpu as pltpu
from jax.sharding import PartitionSpec as P

EPS = 1e-06
ROPE_BASE = 1000000.0
HEAD = 128
GROUP = 4
STEPS = 4
SCALE2 = math.log2(math.e) / math.sqrt(HEAD)
NEG = -1e30
CHUNK = 1024
Y_ORDER = (1, 3, 2)
STEPS_Z = (
    ((3, 0, 1, 2), (1, 2, 3, 0)),
    ((2, 3, 0, 1), (2, 3, 0, 1)),
    ((1, 2, 3, 0), (3, 0, 1, 2)),
)
F32 = jnp.float32
BF16 = jnp.bfloat16
MIB = 1024 * 1024


def dot(a, b):
    return lax.dot_general(a, b, (((1,), (0,)), ((), ())), preferred_element_type=F32)


def dot_t(a, b):
    return lax.dot_general(a, b, (((1,), (1,)), ((), ())), preferred_element_type=F32)


def rms(rows, gain):
    factor = lax.rsqrt(jnp.mean(rows * rows, axis=-1, keepdims=True) + EPS)
    return rows * factor * gain


def rope_tables(positions):
    lane = lax.broadcasted_iota(jnp.int32, positions.shape, 1)
    exponent = (lane % (HEAD // 2)).astype(F32) * (2.0 / HEAD)
    angles = positions * jnp.exp(-math.log(ROPE_BASE) * exponent)
    sine = jnp.sin(angles)
    return jnp.cos(angles), jnp.where(lane < HEAD // 2, -sine, sine)


def rotate(v, cosine, sine):
    return v * cosine + pltpu.roll(v, HEAD // 2, 1) * sine


def decode_kernel(
    lengths, decode_in, embed, norm_gain, query_gain, key_gain, w_query, w_key, w_value, w_out,
    keys, values, dterms, dkey, dvalue, cos_out, sin_out,
):
    path = lax.axis_index("path")
    len0 = lengths[path * 2]
    len1 = lengths[path * 2 + 1]
    hidden = jnp.concatenate(
        [decode_in[i].astype(F32) + embed[i : i + 1, :].astype(F32) for i in range(2)], axis=0
    )
    normed = rms(hidden, norm_gain[...].astype(F32)).astype(BF16)
    row = lax.broadcasted_iota(jnp.int32, (8, HEAD), 0)
    position = jnp.where(row < STEPS, len0 + row, len1 + row - STEPS).astype(F32)
    cosine, sine = rope_tables(position)
    rows = cos_out.shape[0]
    row = lax.broadcasted_iota(jnp.int32, (rows, HEAD), 0)
    cos_all, sin_all = rope_tables((keys.shape[1] + path * rows + row).astype(F32))
    cos_out[...] = cos_all
    sin_out[...] = sin_all
    query = dot(normed, w_query[...])
    qgain = query_gain[...].astype(F32)
    heads = [
        rotate(rms(query[:, h * HEAD : (h + 1) * HEAD], qgain), cosine, sine)
        for h in range(GROUP)
    ]
    new_key = rotate(rms(dot(normed, w_key[...]), key_gain[...].astype(F32)), cosine, sine)
    new_key = new_key.astype(BF16)
    new_value = dot(normed, w_value[...]).astype(BF16)
    dkey[...] = new_key.astype(F32)
    dvalue[...] = new_value.astype(F32)
    mixed = []
    for i, length in enumerate((len0, len1)):
        q = jnp.concatenate([x[i * STEPS : (i + 1) * STEPS] for x in heads], axis=0).astype(BF16)
        cached = dot_t(q, keys[i])
        slot = lax.broadcasted_iota(jnp.int32, cached.shape, 1)
        cached = jnp.where(slot < length, cached, NEG)
        recent = dot_t(q, new_key)
        r_row = lax.broadcasted_iota(jnp.int32, recent.shape, 0) % STEPS
        r_col = lax.broadcasted_iota(jnp.int32, recent.shape, 1) - i * STEPS
        recent = jnp.where((r_col >= 0) & (r_col <= r_row), recent, NEG)
        peak = jnp.maximum(
            jnp.max(cached, axis=-1, keepdims=True), jnp.max(recent, axis=-1, keepdims=True)
        )
        wc = jnp.exp2((cached - peak) * SCALE2)
        wr = jnp.exp2((recent - peak) * SCALE2)
        total = jnp.sum(wc, axis=-1, keepdims=True) + jnp.sum(wr, axis=-1, keepdims=True)
        mix = dot(wc.astype(BF16), values[i]) + dot(wr.astype(BF16), new_value)
        mix = mix / total
        mixed.append(
            jnp.concatenate([mix[h * STEPS : (h + 1) * STEPS] for h in range(GROUP)], axis=1)
        )
    attn = jnp.concatenate(mixed, axis=0).astype(BF16)
    width = dterms.shape[2]
    for t in range(dterms.shape[0]):
        dterms[t] = dot(attn, w_out[:, t * width : (t + 1) * width]).astype(BF16)


def hold_kernel(rows, out):
    out[...] = rows[...]


def norm_kernel(rows0, rows1, rows2, rows3, gain, dkey, dvalue, out, tail_key, tail_value):
    for k, ref in enumerate((rows0, rows1, rows2, rows3)):
        out[k] = rms(ref[...].astype(F32), gain[...].astype(F32)).astype(BF16)
    tail_key[...] = dkey[...]
    tail_value[...] = dvalue[...]


def project_kernel(
    mine, other, query_gain, key_gain, w_query, w_key, w_value, cosine, sine, dkey, dvalue,
    query_out, tail_keys, tail_values, normed_f32,
):
    own = lax.axis_index("tensor")
    for k in range(4):
        for flipped, ref in ((0, mine), (1, other)):
            at = pl.multiple_of((2 * ((own // 2 + 4 - k) % 4) + (own % 2 ^ flipped)) * 8, 8)
            normed_f32[pl.ds(at, 8), :] = ref[k].astype(F32)
    normed = normed_f32[...].astype(BF16)
    cos = cosine[...]
    sin = sine[...]
    query = dot(normed, w_query[...])
    qgain = query_gain[...].astype(F32)
    for h in range(GROUP):
        at = slice(h * HEAD, (h + 1) * HEAD)
        query_out[:, at] = rotate(rms(query[:, at], qgain), cos, sin).astype(BF16)
    key = rotate(rms(dot(normed, w_key[...]), key_gain[...].astype(F32)), cos, sin)
    value = dot(normed, w_value[...])
    pad = jnp.zeros((56, HEAD), F32)
    tail_keys[...] = jnp.concatenate([key, dkey[...], pad], axis=0).astype(BF16)
    tail_values[...] = jnp.concatenate([value, dvalue[...], pad], axis=0).astype(BF16)


def attend_kernel(
    step, lengths, query, keys, values, tail_keys, tail_values, _, out
):
    path = lax.axis_index("path")
    core = lax.axis_index("tensor") % 2
    block = jnp.int32(0)
    for c, table in enumerate(STEPS_Z[step] if step >= 0 else (range(4),) * 2):
        for p, b in enumerate(table):
            block = jnp.where((path == p) & (core == c), b, block)
    rows = out.shape[0]
    q = jnp.concatenate([query[:, h * HEAD : (h + 1) * HEAD] for h in range(GROUP)], axis=0)
    chunks = [(i, c) for i in range(2) for c in range(0, keys.shape[1], CHUNK)]

    def tail_scores():
        s = dot_t(q, tail_keys[...])
        col = lax.broadcasted_iota(jnp.int32, s.shape, 1)
        row = lax.broadcasted_iota(jnp.int32, s.shape, 0) % rows
        causal = (col < rows) & (path * rows + col <= block * rows + row)
        recent = (col >= rows) & (col < rows + 8)
        return jnp.where(causal | recent, s, NEG)

    def chunk_scores(i, c):
        s = dot_t(q, keys[i, c : c + CHUNK, :])
        slot = lax.broadcasted_iota(jnp.int32, (1, CHUNK), 1) + c
        return s + jnp.where(slot < lengths[path * 2 + i], 0.0, NEG)

    scores = tail_scores()
    peak = jnp.max(scores, axis=-1, keepdims=True) * SCALE2
    coming = chunk_scores(*chunks[0])
    w = jnp.exp2(scores * SCALE2 - peak)
    total = jnp.sum(w, axis=-1, keepdims=True)
    mix = dot(w.astype(BF16), tail_values[...])
    for n, (i, c) in enumerate(chunks):
        scores = coming
        if n + 1 < len(chunks):
            coming = chunk_scores(*chunks[n + 1])
        higher = jnp.maximum(peak, jnp.max(scores, axis=-1, keepdims=True) * SCALE2)
        fade = jnp.exp2(peak - higher)
        w = jnp.exp2(scores * SCALE2 - higher)
        total = total * fade + jnp.sum(w, axis=-1, keepdims=True)
        mix = mix * fade + dot(w.astype(BF16), values[i, c : c + CHUNK, :])
        peak = higher
    rounded = peak.astype(BF16).astype(F32)
    fade = jnp.exp2(peak - rounded)
    write_part(out, rows, mix * fade, rounded, total * fade)


def write_part(out, rows, mix, peak, total):
    high = total.astype(BF16).astype(F32)
    low = total - high
    lane = lax.broadcasted_iota(jnp.int32, (rows, HEAD), 1)
    stats = jnp.zeros((rows, HEAD), F32)
    for h in range(GROUP):
        at = slice(h * rows, (h + 1) * rows)
        out[:, h * HEAD : (h + 1) * HEAD] = mix[at].astype(BF16)
        for n, x in enumerate((peak, high, low)):
            stats = jnp.where(lane == n * GROUP + h, x[at], stats)
    out[:, GROUP * HEAD :] = stats.astype(BF16)


def merge(parts):
    mixes = []
    totals = []
    peak = functools.reduce(jnp.maximum, [p for _, p, _ in parts])
    scales = [jnp.exp2(p - peak) for _, p, _ in parts]
    total = sum(w * t for w, (_, _, t) in zip(scales, parts))
    for h in range(GROUP):
        at = slice(h * HEAD, (h + 1) * HEAD)
        mixes.append(sum(w[:, h : h + 1] * x[:, at] for w, (x, _, _) in zip(scales, parts)))
    return mixes, peak, total


def read_part(part):
    width = GROUP * HEAD
    stats = part[:, width:].astype(F32)
    total = stats[:, GROUP : 2 * GROUP] + stats[:, 2 * GROUP : 3 * GROUP]
    return part[:, :width].astype(F32), stats[:, :GROUP], total


def project_half(attn, which, w_out, dterms, ref):
    width = w_out.shape[1]
    lhs = jnp.concatenate(
        [attn[pl.ds(pl.multiple_of((2 * y + which) * 8, 8), 8), :] for y in range(4)], axis=0
    ).astype(BF16)
    res = dot(lhs, w_out[...])
    for y in range(4):
        ref[y, :, :width] = res[y * 8 : (y + 1) * 8].astype(ref.dtype)
        ref[y, :, width:] = dterms[2 * y + which].astype(ref.dtype)


def send_kernel(own_part, part1, part2, part3, w_out, dterms, send, attn):
    core = lax.axis_index("tensor") % 2
    parts = (own_part[...], part1[...], part2[...], part3[...])
    mixes, _, total = merge([read_part(x) for x in parts])
    for h in range(GROUP):
        attn[:, h * HEAD : (h + 1) * HEAD] = mixes[h] / total[:, h : h + 1]
    project_half(attn, 1 - core, w_out, dterms, send)


def keep_kernel(attn, w_out, dterms, keep):
    project_half(attn, lax.axis_index("tensor") % 2, w_out, dterms, keep)


def fold_kernel(keep, received, own_out, out1, out2, out3):
    at = lax.axis_index("tensor") // 2
    for k, ref in enumerate((own_out, out1, out2, out3)):
        block = (at + k) % 4
        ref[...] = (keep[block] + received[block].astype(F32)).astype(ref.dtype)


def final_kernel(own, in1, in2, in3, decode_out, summary_out):
    total = own[...] + in1[...].astype(F32) + in2[...].astype(F32) + in3[...].astype(F32)
    width = summary_out.shape[1]
    summary_out[...] = total[:, :width].astype(BF16)
    decode_out[0] = total[:STEPS, width:].astype(BF16)
    decode_out[1] = total[STEPS:, width:].astype(BF16)


def call(kernel, out_shape, args, scratch=(), limit=32, flops=0, smem=(), far=(), nbytes=None):
    specs = [
        pl.BlockSpec(
            memory_space=pltpu.SMEM if i in smem else pltpu.HBM if i in far else pltpu.VMEM
        )
        for i in range(len(args))
    ]
    if nbytes is None:
        nbytes = sum(math.prod(a.shape) * a.dtype.itemsize for a in args)
    outs = tuple(jax.ShapeDtypeStruct(s, d) for s, d in out_shape)
    out = pl.pallas_call(
        kernel,
        out_shape=outs,
        in_specs=specs,
        out_specs=tuple(pl.BlockSpec(memory_space=pltpu.VMEM) for _ in outs),
        scratch_shapes=list(scratch),
        compiler_params=pltpu.CompilerParams(vmem_limit_bytes=limit * MIB),
        cost_estimate=pl.CostEstimate(flops=flops, bytes_accessed=nbytes, transcendentals=0),
    )(*args)
    return out


def flip(x, axis, size, k):
    return lax.ppermute(x, axis, [(i, i ^ k) for i in range(size)])


def shift(x, axis, size, k):
    return lax.ppermute(x, axis, [(i, (i + k) % size) for i in range(size)])


def routes(step):
    return [
        (p * 8 + t, STEPS_Z[step][t % 2][p] * 8 + t) for p in range(4) for t in range(8)
    ]


def fetch(x, step):
    return lax.ppermute(x, ("path", "tensor"), [(b, a) for a, b in routes(step)])


def give_back(x, step):
    return lax.ppermute(x, ("path", "tensor"), routes(step))


def body(
    decode_in,
    path_embed,
    summary_in,
    norm_gain,
    query_gain,
    key_norm_gain,
    w_query,
    key_weight,
    w_value,
    w_out,
    key_cache,
    value_cache,
    lengths,
):
    width = w_out.shape[1]
    rows = 64
    norm_gain = norm_gain.reshape(1, -1)
    query_gain = query_gain.reshape(1, -1)
    key_gain = key_norm_gain.reshape(1, -1)

    (own_rows,) = call(hold_kernel, [(summary_in.shape, BF16)], (summary_in,), flops=10**10)
    across = {0: own_rows}
    for k in Y_ORDER:
        across[k] = shift(own_rows, "tensor", 8, 2 * k)
    across = [across[k] for k in range(4)]

    dterms, dkey, dvalue, cosine, sine = call(
        decode_kernel,
        [((8, 8, width // 8), BF16), ((8, HEAD), F32), ((8, HEAD), F32), ((rows, HEAD), F32), ((rows, HEAD), F32)],
        (lengths, decode_in, path_embed, norm_gain, query_gain, key_gain, w_query, key_weight,
         w_value, w_out, key_cache, value_cache),
        limit=24,
        smem=(0,),
        flops=6 * 10**9,
    )

    mine, dkey, dvalue = call(
        norm_kernel,
        [((4, 8, width), BF16), ((8, HEAD), F32), ((8, HEAD), F32)],
        (*across, norm_gain, dkey, dvalue),
    )
    other = flip(mine, "tensor", 8, 1)
    query, *tails = call(
        project_kernel,
        [((rows, GROUP * HEAD), BF16), ((128, HEAD), BF16), ((128, HEAD), BF16)],
        (mine, other, query_gain, key_gain, w_query, key_weight, w_value, cosine, sine, dkey, dvalue),
        scratch=[pltpu.VMEM((rows, width), F32)],
        limit=24,
        flops=2 * 64 * 4096 * 768,
    )
    queries = {-1: query}
    for n in range(3):
        queries[n] = fetch(query, n)

    def attend(k, after):
        (part,) = call(
            functools.partial(attend_kernel, k),
            [((rows, (GROUP + 1) * HEAD), BF16)],
            (lengths, queries[k], key_cache, value_cache, *tails, after),
            limit=24,
            smem=(0,),
            flops=3 * 10**9,
        )
        return part

    parts = []
    last = query
    for n in range(3):
        last = attend(n, last)
        parts.append(give_back(last, n))
    parts.append(attend(-1, last))

    send, attn = call(
        send_kernel,
        [((4, 8, width + width // 8), BF16), ((rows, GROUP * HEAD), F32)],
        (*parts, w_out, dterms),
        limit=24,
        flops=64 * 512 * 4096,
    )
    received = flip(send, "tensor", 8, 1)
    (keep,) = call(
        keep_kernel,
        [((4, 8, width + width // 8), F32)],
        (attn, w_out, dterms),
        limit=24,
        flops=64 * 512 * 4096,
    )
    own, out1, out2, out3 = call(
        fold_kernel,
        [((8, width + width // 8), F32)] + [((8, width + width // 8), BF16)] * 3,
        (keep, received),
    )
    outs = {1: out1, 2: out2, 3: out3}
    ins = {k: shift(outs[k], "tensor", 8, 2 * k) for k in Y_ORDER}
    decode_out, summary_out = call(
        final_kernel,
        [((2, STEPS, width // 8), BF16), ((8, width), BF16)],
        (own, ins[1], ins[2], ins[3]),
    )
    return (decode_out, summary_out)


def solution(mesh):
    in_specs = (
        P(("problem", "path"), None, None),
        P("path", None),
        P(("problem", "path", "tensor"), None),
        P(),
        P(),
        P(),
        P(None, "tensor"),
        P(None, "tensor"),
        P(None, "tensor"),
        P("tensor", None),
        P(("problem", "path"), None, "tensor"),
        P(("problem", "path"), None, "tensor"),
        P("problem"),
    )
    out_specs = (P(("problem", "path"), None, "tensor"), P(("problem", "path", "tensor"), None))
    return jax.shard_map(body, mesh=mesh, in_specs=in_specs, out_specs=out_specs, check_vma=False)
```

```python
import functools
import math

import jax
import jax.numpy as jnp
from jax import lax
from jax.experimental import pallas as pl
from jax.experimental.pallas import tpu as pltpu
from jax.sharding import PartitionSpec as P

EPS = 1e-06
ROPE_BASE = 1000000.0
HEAD = 128
GROUP = 4
STEPS = 4
SCALE2 = math.log2(math.e) / math.sqrt(HEAD)
NEG = -1e30
CHUNK = 1024
Y_ORDER = (1, 3, 2)
STEPS_Z = (
    ((3, 0, 1, 2), (1, 2, 3, 0)),
    ((2, 3, 0, 1), (2, 3, 0, 1)),
    ((1, 2, 3, 0), (3, 0, 1, 2)),
)
F32 = jnp.float32
BF16 = jnp.bfloat16
MIB = 1024 * 1024


def dot(a, b):
    return lax.dot_general(a, b, (((1,), (0,)), ((), ())), preferred_element_type=F32)


def dot_t(a, b):
    return lax.dot_general(a, b, (((1,), (1,)), ((), ())), preferred_element_type=F32)


def rms(rows, gain):
    factor = lax.rsqrt(jnp.mean(rows * rows, axis=-1, keepdims=True) + EPS)
    return rows * factor * gain


def rope_tables(positions):
    lane = lax.broadcasted_iota(jnp.int32, positions.shape, 1)
    exponent = (lane % (HEAD // 2)).astype(F32) * (2.0 / HEAD)
    angles = positions * jnp.exp(-math.log(ROPE_BASE) * exponent)
    sine = jnp.sin(angles)
    return jnp.cos(angles), jnp.where(lane < HEAD // 2, -sine, sine)


def rotate(v, cosine, sine):
    return v * cosine + pltpu.roll(v, HEAD // 2, 1) * sine


def decode_kernel(
    lengths, decode_in, embed, norm_gain, query_gain, key_gain, w_query, w_key, w_value, w_out,
    keys, values, dterms, dkey, dvalue, cos_out, sin_out,
):
    path = lax.axis_index("path")
    len0 = lengths[path * 2]
    len1 = lengths[path * 2 + 1]
    hidden = jnp.concatenate(
        [decode_in[i].astype(F32) + embed[i : i + 1, :].astype(F32) for i in range(2)], axis=0
    )
    normed = rms(hidden, norm_gain[...].astype(F32)).astype(BF16)
    row = lax.broadcasted_iota(jnp.int32, (8, HEAD), 0)
    position = jnp.where(row < STEPS, len0 + row, len1 + row - STEPS).astype(F32)
    cosine, sine = rope_tables(position)
    rows = cos_out.shape[0]
    row = lax.broadcasted_iota(jnp.int32, (rows, HEAD), 0)
    cos_all, sin_all = rope_tables((keys.shape[1] + path * rows + row).astype(F32))
    cos_out[...] = cos_all
    sin_out[...] = sin_all
    query = dot(normed, w_query[...])
    qgain = query_gain[...].astype(F32)
    heads = [
        rotate(rms(query[:, h * HEAD : (h + 1) * HEAD], qgain), cosine, sine)
        for h in range(GROUP)
    ]
    new_key = rotate(rms(dot(normed, w_key[...]), key_gain[...].astype(F32)), cosine, sine)
    new_key = new_key.astype(BF16)
    new_value = dot(normed, w_value[...]).astype(BF16)
    dkey[...] = new_key.astype(F32)
    dvalue[...] = new_value.astype(F32)
    mixed = []
    for i, length in enumerate((len0, len1)):
        q = jnp.concatenate([x[i * STEPS : (i + 1) * STEPS] for x in heads], axis=0).astype(BF16)
        cached = dot_t(q, keys[i])
        slot = lax.broadcasted_iota(jnp.int32, cached.shape, 1)
        cached = jnp.where(slot < length, cached, NEG)
        recent = dot_t(q, new_key)
        r_row = lax.broadcasted_iota(jnp.int32, recent.shape, 0) % STEPS
        r_col = lax.broadcasted_iota(jnp.int32, recent.shape, 1) - i * STEPS
        recent = jnp.where((r_col >= 0) & (r_col <= r_row), recent, NEG)
        peak = jnp.maximum(
            jnp.max(cached, axis=-1, keepdims=True), jnp.max(recent, axis=-1, keepdims=True)
        )
        wc = jnp.exp2((cached - peak) * SCALE2)
        wr = jnp.exp2((recent - peak) * SCALE2)
        total = jnp.sum(wc, axis=-1, keepdims=True) + jnp.sum(wr, axis=-1, keepdims=True)
        mix = dot(wc.astype(BF16), values[i]) + dot(wr.astype(BF16), new_value)
        mix = mix / total
        mixed.append(
            jnp.concatenate([mix[h * STEPS : (h + 1) * STEPS] for h in range(GROUP)], axis=1)
        )
    attn = jnp.concatenate(mixed, axis=0).astype(BF16)
    width = dterms.shape[2]
    for t in range(dterms.shape[0]):
        dterms[t] = dot(attn, w_out[:, t * width : (t + 1) * width]).astype(BF16)


def begin_kernel(out):
    out[...] = jnp.zeros_like(out)


def hold_kernel(rows, _, out):
    out[...] = rows[...]


def norm_kernel(rows0, rows1, rows2, rows3, gain, dkey, dvalue, out, tail_key, tail_value):
    for k, ref in enumerate((rows0, rows1, rows2, rows3)):
        out[k] = rms(ref[...].astype(F32), gain[...].astype(F32)).astype(BF16)
    tail_key[...] = dkey[...]
    tail_value[...] = dvalue[...]


def project_kernel(
    mine, other, query_gain, w_query, cosine, sine, query_out, normed_out, normed_f32
):
    own = lax.axis_index("tensor")
    for k in range(4):
        for flipped, ref in ((0, mine), (1, other)):
            at = pl.multiple_of((2 * ((own // 2 + 4 - k) % 4) + (own % 2 ^ flipped)) * 8, 8)
            normed_f32[pl.ds(at, 8), :] = ref[k].astype(F32)
    normed = normed_f32[...].astype(BF16)
    normed_out[...] = normed
    query = dot(normed, w_query[...])
    qgain = query_gain[...].astype(F32)
    for h in range(GROUP):
        at = slice(h * HEAD, (h + 1) * HEAD)
        query_out[:, at] = rotate(rms(query[:, at], qgain), cosine[...], sine[...]).astype(BF16)


def tail_kernel(
    normed, key_gain, w_key, w_value, cosine, sine, dkey, dvalue, tail_keys, tail_values
):
    rows = normed[...]
    key = rms(dot(rows, w_key[...]), key_gain[...].astype(F32))
    key = rotate(key, cosine[...], sine[...])
    value = dot(rows, w_value[...])
    pad = jnp.zeros((56, HEAD), F32)
    tail_keys[...] = jnp.concatenate([key, dkey[...], pad], axis=0).astype(BF16)
    tail_values[...] = jnp.concatenate([value, dvalue[...], pad], axis=0).astype(BF16)


def attend_kernel(
    step, lengths, query, keys, values, tail_keys, tail_values, _, out
):
    path = lax.axis_index("path")
    core = lax.axis_index("tensor") % 2
    block = jnp.int32(0)
    for c, table in enumerate(STEPS_Z[step] if step >= 0 else (range(4),) * 2):
        for p, b in enumerate(table):
            block = jnp.where((path == p) & (core == c), b, block)
    rows = out.shape[0]
    q = jnp.concatenate([query[:, h * HEAD : (h + 1) * HEAD] for h in range(GROUP)], axis=0)
    chunks = [(i, c) for i in range(2) for c in range(0, keys.shape[1], CHUNK)]

    def tail_scores():
        s = dot_t(q, tail_keys[...])
        col = lax.broadcasted_iota(jnp.int32, s.shape, 1)
        row = lax.broadcasted_iota(jnp.int32, s.shape, 0) % rows
        causal = (col < rows) & (path * rows + col <= block * rows + row)
        recent = (col >= rows) & (col < rows + 8)
        return jnp.where(causal | recent, s, NEG)

    def chunk_scores(i, c):
        s = dot_t(q, keys[i, c : c + CHUNK, :])
        slot = lax.broadcasted_iota(jnp.int32, (1, CHUNK), 1) + c
        return s + jnp.where(slot < lengths[path * 2 + i], 0.0, NEG)

    scores = tail_scores()
    peak = jnp.max(scores, axis=-1, keepdims=True) * SCALE2
    coming = chunk_scores(*chunks[0])
    w = jnp.exp2(scores * SCALE2 - peak)
    total = jnp.sum(w, axis=-1, keepdims=True)
    mix = dot(w.astype(BF16), tail_values[...])
    for n, (i, c) in enumerate(chunks):
        scores = coming
        if n + 1 < len(chunks):
            coming = chunk_scores(*chunks[n + 1])
        higher = jnp.maximum(peak, jnp.max(scores, axis=-1, keepdims=True) * SCALE2)
        fade = jnp.exp2(peak - higher)
        w = jnp.exp2(scores * SCALE2 - higher)
        total = total * fade + jnp.sum(w, axis=-1, keepdims=True)
        mix = mix * fade + dot(w.astype(BF16), values[i, c : c + CHUNK, :])
        peak = higher
    rounded = peak.astype(BF16).astype(F32)
    fade = jnp.exp2(peak - rounded)
    write_part(out, rows, mix * fade, rounded, total * fade)


def write_part(out, rows, mix, peak, total):
    high = total.astype(BF16).astype(F32)
    low = total - high
    lane = lax.broadcasted_iota(jnp.int32, (rows, HEAD), 1)
    stats = jnp.zeros((rows, HEAD), F32)
    for h in range(GROUP):
        at = slice(h * rows, (h + 1) * rows)
        out[:, h * HEAD : (h + 1) * HEAD] = mix[at].astype(BF16)
        for n, x in enumerate((peak, high, low)):
            stats = jnp.where(lane == n * GROUP + h, x[at], stats)
    out[:, GROUP * HEAD :] = stats.astype(BF16)


def merge(parts):
    mixes = []
    totals = []
    peak = functools.reduce(jnp.maximum, [p for _, p, _ in parts])
    scales = [jnp.exp2(p - peak) for _, p, _ in parts]
    total = sum(w * t for w, (_, _, t) in zip(scales, parts))
    for h in range(GROUP):
        at = slice(h * HEAD, (h + 1) * HEAD)
        mixes.append(sum(w[:, h : h + 1] * x[:, at] for w, (x, _, _) in zip(scales, parts)))
    return mixes, peak, total


def read_part(part):
    width = GROUP * HEAD
    stats = part[:, width:].astype(F32)
    total = stats[:, GROUP : 2 * GROUP] + stats[:, 2 * GROUP : 3 * GROUP]
    return part[:, :width].astype(F32), stats[:, :GROUP], total


def project_half(attn, which, w_out, dterms, ref):
    width = w_out.shape[1]
    lhs = jnp.concatenate(
        [attn[pl.ds(pl.multiple_of((2 * y + which) * 8, 8), 8), :] for y in range(4)], axis=0
    ).astype(BF16)
    res = dot(lhs, w_out[...])
    for y in range(4):
        ref[y, :, :width] = res[y * 8 : (y + 1) * 8].astype(ref.dtype)
        ref[y, :, width:] = dterms[2 * y + which].astype(ref.dtype)


def send_kernel(own_part, part1, part2, part3, w_out, dterms, send, attn):
    core = lax.axis_index("tensor") % 2
    parts = (own_part[...], part1[...], part2[...], part3[...])
    mixes, _, total = merge([read_part(x) for x in parts])
    for h in range(GROUP):
        attn[:, h * HEAD : (h + 1) * HEAD] = mixes[h] / total[:, h : h + 1]
    project_half(attn, 1 - core, w_out, dterms, send)


def keep_kernel(attn, w_out, dterms, keep):
    project_half(attn, lax.axis_index("tensor") % 2, w_out, dterms, keep)


def fold_kernel(keep, received, own_out, out1, out2, out3):
    at = lax.axis_index("tensor") // 2
    for k, ref in enumerate((own_out, out1, out2, out3)):
        block = (at + k) % 4
        ref[...] = (keep[block] + received[block].astype(F32)).astype(ref.dtype)


def final_kernel(own, in1, in2, in3, decode_out, summary_out):
    total = own[...] + in1[...].astype(F32) + in2[...].astype(F32) + in3[...].astype(F32)
    width = summary_out.shape[1]
    summary_out[...] = total[:, :width].astype(BF16)
    decode_out[0] = total[:STEPS, width:].astype(BF16)
    decode_out[1] = total[STEPS:, width:].astype(BF16)


def call(kernel, out_shape, args, scratch=(), limit=32, flops=0, smem=(), far=(), nbytes=None):
    specs = [
        pl.BlockSpec(
            memory_space=pltpu.SMEM if i in smem else pltpu.HBM if i in far else pltpu.VMEM
        )
        for i in range(len(args))
    ]
    if nbytes is None:
        nbytes = sum(math.prod(a.shape) * a.dtype.itemsize for a in args)
    outs = tuple(jax.ShapeDtypeStruct(s, d) for s, d in out_shape)
    out = pl.pallas_call(
        kernel,
        out_shape=outs,
        in_specs=specs,
        out_specs=tuple(pl.BlockSpec(memory_space=pltpu.VMEM) for _ in outs),
        scratch_shapes=list(scratch),
        compiler_params=pltpu.CompilerParams(vmem_limit_bytes=limit * MIB),
        cost_estimate=pl.CostEstimate(flops=flops, bytes_accessed=nbytes, transcendentals=0),
    )(*args)
    return out


def flip(x, axis, size, k):
    return lax.ppermute(x, axis, [(i, i ^ k) for i in range(size)])


def shift(x, axis, size, k):
    return lax.ppermute(x, axis, [(i, (i + k) % size) for i in range(size)])


def routes(step):
    return [
        (p * 8 + t, STEPS_Z[step][t % 2][p] * 8 + t) for p in range(4) for t in range(8)
    ]


def fetch(x, step):
    return lax.ppermute(x, ("path", "tensor"), [(b, a) for a, b in routes(step)])


def give_back(x, step):
    return lax.ppermute(x, ("path", "tensor"), routes(step))


def body(
    decode_in,
    path_embed,
    summary_in,
    norm_gain,
    query_gain,
    key_norm_gain,
    w_query,
    key_weight,
    w_value,
    w_out,
    key_cache,
    value_cache,
    lengths,
):
    width = w_out.shape[1]
    rows = 64
    norm_gain = norm_gain.reshape(1, -1)
    query_gain = query_gain.reshape(1, -1)
    key_gain = key_norm_gain.reshape(1, -1)

    (begun,) = call(begin_kernel, [((8, HEAD), F32)], (), flops=10**10)
    (own_rows,) = call(hold_kernel, [(summary_in.shape, BF16)], (summary_in, begun))
    across = {0: own_rows}
    for k in Y_ORDER:
        across[k] = shift(own_rows, "tensor", 8, 2 * k)
    across = [across[k] for k in range(4)]

    dterms, dkey, dvalue, cosine, sine = call(
        decode_kernel,
        [((8, 8, width // 8), BF16), ((8, HEAD), F32), ((8, HEAD), F32), ((rows, HEAD), F32), ((rows, HEAD), F32)],
        (lengths, decode_in, path_embed, norm_gain, query_gain, key_gain, w_query, key_weight,
         w_value, w_out, key_cache, value_cache),
        limit=24,
        smem=(0,),
        flops=6 * 10**9,
    )

    mine, dkey, dvalue = call(
        norm_kernel,
        [((4, 8, width), BF16), ((8, HEAD), F32), ((8, HEAD), F32)],
        (*across, norm_gain, dkey, dvalue),
    )
    other = flip(mine, "tensor", 8, 1)
    query, normed = call(
        project_kernel,
        [((rows, GROUP * HEAD), BF16), ((rows, width), BF16)],
        (mine, other, query_gain, w_query, cosine, sine),
        scratch=[pltpu.VMEM((rows, width), F32)],
        limit=24,
        flops=2 * 64 * 4096 * 512,
    )
    queries = {-1: query}
    for n in range(3):
        queries[n] = fetch(query, n)
    tails = call(
        tail_kernel,
        [((128, HEAD), BF16), ((128, HEAD), BF16)],
        (normed, key_gain, key_weight, w_value, cosine, sine, dkey, dvalue),
        limit=24,
        flops=2 * 64 * 4096 * 256,
    )

    def attend(k, after):
        (part,) = call(
            functools.partial(attend_kernel, k),
            [((rows, (GROUP + 1) * HEAD), BF16)],
            (lengths, queries[k], key_cache, value_cache, *tails, after),
            limit=24,
            smem=(0,),
            flops=3 * 10**9,
        )
        return part

    parts = []
    last = query
    for n in range(3):
        last = attend(n, last)
        parts.append(give_back(last, n))
    parts.append(attend(-1, last))

    send, attn = call(
        send_kernel,
        [((4, 8, width + width // 8), BF16), ((rows, GROUP * HEAD), F32)],
        (*parts, w_out, dterms),
        limit=24,
        flops=64 * 512 * 4096,
    )
    received = flip(send, "tensor", 8, 1)
    (keep,) = call(
        keep_kernel,
        [((4, 8, width + width // 8), F32)],
        (attn, w_out, dterms),
        limit=24,
        flops=64 * 512 * 4096,
    )
    own, out1, out2, out3 = call(
        fold_kernel,
        [((8, width + width // 8), F32)] + [((8, width + width // 8), BF16)] * 3,
        (keep, received),
    )
    outs = {1: out1, 2: out2, 3: out3}
    ins = {k: shift(outs[k], "tensor", 8, 2 * k) for k in Y_ORDER}
    decode_out, summary_out = call(
        final_kernel,
        [((2, STEPS, width // 8), BF16), ((8, width), BF16)],
        (own, ins[1], ins[2], ins[3]),
    )
    return (decode_out, summary_out)


def solution(mesh):
    in_specs = (
        P(("problem", "path"), None, None),
        P("path", None),
        P(("problem", "path", "tensor"), None),
        P(),
        P(),
        P(),
        P(None, "tensor"),
        P(None, "tensor"),
        P(None, "tensor"),
        P("tensor", None),
        P(("problem", "path"), None, "tensor"),
        P(("problem", "path"), None, "tensor"),
        P("problem"),
    )
    out_specs = (P(("problem", "path"), None, "tensor"), P(("problem", "path", "tensor"), None))
    return jax.shard_map(body, mesh=mesh, in_specs=in_specs, out_specs=out_specs, check_vma=False)
```

```python
import functools
import math

import jax
import jax.numpy as jnp
from jax import lax
from jax.experimental import pallas as pl
from jax.experimental.pallas import tpu as pltpu
from jax.sharding import PartitionSpec as P

EPS = 1e-06
ROPE_BASE = 1000000.0
HEAD = 128
GROUP = 4
STEPS = 4
SCALE2 = math.log2(math.e) / math.sqrt(HEAD)
NEG = -1e30
CHUNK = 1024
Y_ORDER = (1, 3, 2)
STEPS_Z = (
    ((3, 0, 1, 2), (1, 2, 3, 0)),
    ((2, 3, 0, 1), (2, 3, 0, 1)),
    ((1, 2, 3, 0), (3, 0, 1, 2)),
)
F32 = jnp.float32
BF16 = jnp.bfloat16
MIB = 1024 * 1024


def dot(a, b):
    return lax.dot_general(a, b, (((1,), (0,)), ((), ())), preferred_element_type=F32)


def dot_t(a, b):
    return lax.dot_general(a, b, (((1,), (1,)), ((), ())), preferred_element_type=F32)


def rms(rows, gain):
    factor = lax.rsqrt(jnp.mean(rows * rows, axis=-1, keepdims=True) + EPS)
    return rows * factor * gain


def rope_tables(positions):
    lane = lax.broadcasted_iota(jnp.int32, positions.shape, 1)
    exponent = (lane % (HEAD // 2)).astype(F32) * (2.0 / HEAD)
    angles = positions * jnp.exp(-math.log(ROPE_BASE) * exponent)
    sine = jnp.sin(angles)
    return jnp.cos(angles), jnp.where(lane < HEAD // 2, -sine, sine)


def rotate(v, cosine, sine):
    return v * cosine + pltpu.roll(v, HEAD // 2, 1) * sine


def decode_kernel(
    lengths, decode_in, embed, norm_gain, query_gain, key_gain, w_query, w_key, w_value, w_out,
    keys, values, dterms, dkey, dvalue, cos_out, sin_out,
):
    path = lax.axis_index("path")
    len0 = lengths[path * 2]
    len1 = lengths[path * 2 + 1]
    hidden = jnp.concatenate(
        [decode_in[i].astype(F32) + embed[i : i + 1, :].astype(F32) for i in range(2)], axis=0
    )
    normed = rms(hidden, norm_gain[...].astype(F32)).astype(BF16)
    row = lax.broadcasted_iota(jnp.int32, (8, HEAD), 0)
    position = jnp.where(row < STEPS, len0 + row, len1 + row - STEPS).astype(F32)
    cosine, sine = rope_tables(position)
    rows = cos_out.shape[0]
    row = lax.broadcasted_iota(jnp.int32, (rows, HEAD), 0)
    cos_all, sin_all = rope_tables((keys.shape[1] + path * rows + row).astype(F32))
    cos_out[...] = cos_all
    sin_out[...] = sin_all
    query = dot(normed, w_query[...])
    qgain = query_gain[...].astype(F32)
    heads = [
        rotate(rms(query[:, h * HEAD : (h + 1) * HEAD], qgain), cosine, sine)
        for h in range(GROUP)
    ]
    new_key = rotate(rms(dot(normed, w_key[...]), key_gain[...].astype(F32)), cosine, sine)
    new_key = new_key.astype(BF16)
    new_value = dot(normed, w_value[...]).astype(BF16)
    dkey[...] = new_key.astype(F32)
    dvalue[...] = new_value.astype(F32)
    mixed = []
    for i, length in enumerate((len0, len1)):
        q = jnp.concatenate([x[i * STEPS : (i + 1) * STEPS] for x in heads], axis=0).astype(BF16)
        cached = dot_t(q, keys[i])
        slot = lax.broadcasted_iota(jnp.int32, cached.shape, 1)
        cached = jnp.where(slot < length, cached, NEG)
        recent = dot_t(q, new_key)
        r_row = lax.broadcasted_iota(jnp.int32, recent.shape, 0) % STEPS
        r_col = lax.broadcasted_iota(jnp.int32, recent.shape, 1) - i * STEPS
        recent = jnp.where((r_col >= 0) & (r_col <= r_row), recent, NEG)
        peak = jnp.maximum(
            jnp.max(cached, axis=-1, keepdims=True), jnp.max(recent, axis=-1, keepdims=True)
        )
        wc = jnp.exp2((cached - peak) * SCALE2)
        wr = jnp.exp2((recent - peak) * SCALE2)
        total = jnp.sum(wc, axis=-1, keepdims=True) + jnp.sum(wr, axis=-1, keepdims=True)
        mix = dot(wc.astype(BF16), values[i]) + dot(wr.astype(BF16), new_value)
        mix = mix / total
        mixed.append(
            jnp.concatenate([mix[h * STEPS : (h + 1) * STEPS] for h in range(GROUP)], axis=1)
        )
    attn = jnp.concatenate(mixed, axis=0).astype(BF16)
    width = dterms.shape[2]
    for t in range(dterms.shape[0]):
        dterms[t] = dot(attn, w_out[:, t * width : (t + 1) * width]).astype(BF16)


def begin_kernel(out):
    out[...] = jnp.zeros_like(out)


def hold_kernel(rows, _, out):
    out[...] = rows[...]


def norm_kernel(rows0, rows1, rows2, rows3, gain, dkey, dvalue, out, tail_key, tail_value):
    for k, ref in enumerate((rows0, rows1, rows2, rows3)):
        out[k] = rms(ref[...].astype(F32), gain[...].astype(F32)).astype(BF16)
    tail_key[...] = dkey[...]
    tail_value[...] = dvalue[...]


def project_kernel(
    mine, other, query_gain, w_query, cosine, sine, query_out, normed_out, normed_f32
):
    own = lax.axis_index("tensor")
    for k in range(4):
        for flipped, ref in ((0, mine), (1, other)):
            at = pl.multiple_of((2 * ((own // 2 + 4 - k) % 4) + (own % 2 ^ flipped)) * 8, 8)
            normed_f32[pl.ds(at, 8), :] = ref[k].astype(F32)
    normed = normed_f32[...].astype(BF16)
    normed_out[...] = normed
    query = dot(normed, w_query[...])
    qgain = query_gain[...].astype(F32)
    for h in range(GROUP):
        at = slice(h * HEAD, (h + 1) * HEAD)
        query_out[:, at] = rotate(rms(query[:, at], qgain), cosine[...], sine[...]).astype(BF16)


def tail_kernel(
    normed, key_gain, w_key, w_value, cosine, sine, dkey, dvalue, tail_keys, tail_values
):
    rows = normed[...]
    key = rms(dot(rows, w_key[...]), key_gain[...].astype(F32))
    key = rotate(key, cosine[...], sine[...])
    value = dot(rows, w_value[...])
    pad = jnp.zeros((56, HEAD), F32)
    tail_keys[...] = jnp.concatenate([key, dkey[...], pad], axis=0).astype(BF16)
    tail_values[...] = jnp.concatenate([value, dvalue[...], pad], axis=0).astype(BF16)


def attend_kernel(
    step, lengths, query, keys, values, tail_keys, tail_values, _, out
):
    path = lax.axis_index("path")
    core = lax.axis_index("tensor") % 2
    block = jnp.int32(0)
    for c, table in enumerate(STEPS_Z[step] if step >= 0 else (range(4),) * 2):
        for p, b in enumerate(table):
            block = jnp.where((path == p) & (core == c), b, block)
    rows = out.shape[0]
    q = jnp.concatenate([query[:, h * HEAD : (h + 1) * HEAD] for h in range(GROUP)], axis=0)
    chunks = [(i, c) for i in range(2) for c in range(0, keys.shape[1], CHUNK)]

    def tail_scores():
        s = dot_t(q, tail_keys[...])
        col = lax.broadcasted_iota(jnp.int32, s.shape, 1)
        row = lax.broadcasted_iota(jnp.int32, s.shape, 0) % rows
        causal = (col < rows) & (path * rows + col <= block * rows + row)
        recent = (col >= rows) & (col < rows + 8)
        return jnp.where(causal | recent, s, NEG)

    def chunk_scores(i, c):
        s = dot_t(q, keys[i, c : c + CHUNK, :])
        slot = lax.broadcasted_iota(jnp.int32, (1, CHUNK), 1) + c
        return s + jnp.where(slot < lengths[path * 2 + i], 0.0, NEG)

    scores = tail_scores()
    peak = jnp.max(scores, axis=-1, keepdims=True) * SCALE2
    coming = chunk_scores(*chunks[0])
    w = jnp.exp2(scores * SCALE2 - peak)
    total = w
    mix = dot(w.astype(BF16), tail_values[...])
    for n, (i, c) in enumerate(chunks):
        scores = coming
        if n + 1 < len(chunks):
            coming = chunk_scores(*chunks[n + 1])
        higher = jnp.maximum(peak, jnp.max(scores, axis=-1, keepdims=True) * SCALE2)
        fade = jnp.exp2(peak - higher)
        w = jnp.exp2(scores * SCALE2 - higher)
        total = total * fade + sum(w[:, k : k + HEAD] for k in range(0, CHUNK, HEAD))
        mix = mix * fade + dot(w.astype(BF16), values[i, c : c + CHUNK, :])
        peak = higher
    total = jnp.sum(total, axis=-1, keepdims=True)
    rounded = peak.astype(BF16).astype(F32)
    fade = jnp.exp2(peak - rounded)
    write_part(out, rows, mix * fade, rounded, total * fade)


def write_part(out, rows, mix, peak, total):
    high = total.astype(BF16).astype(F32)
    low = total - high
    lane = lax.broadcasted_iota(jnp.int32, (rows, HEAD), 1)
    stats = jnp.zeros((rows, HEAD), F32)
    for h in range(GROUP):
        at = slice(h * rows, (h + 1) * rows)
        out[:, h * HEAD : (h + 1) * HEAD] = mix[at].astype(BF16)
        for n, x in enumerate((peak, high, low)):
            stats = jnp.where(lane == n * GROUP + h, x[at], stats)
    out[:, GROUP * HEAD :] = stats.astype(BF16)


def merge(parts):
    mixes = []
    totals = []
    peak = functools.reduce(jnp.maximum, [p for _, p, _ in parts])
    scales = [jnp.exp2(p - peak) for _, p, _ in parts]
    total = sum(w * t for w, (_, _, t) in zip(scales, parts))
    for h in range(GROUP):
        at = slice(h * HEAD, (h + 1) * HEAD)
        mixes.append(sum(w[:, h : h + 1] * x[:, at] for w, (x, _, _) in zip(scales, parts)))
    return mixes, peak, total


def read_part(part):
    width = GROUP * HEAD
    stats = part[:, width:].astype(F32)
    total = stats[:, GROUP : 2 * GROUP] + stats[:, 2 * GROUP : 3 * GROUP]
    return part[:, :width].astype(F32), stats[:, :GROUP], total


def project_half(attn, which, w_out, dterms, ref):
    width = w_out.shape[1]
    lhs = jnp.concatenate(
        [attn[pl.ds(pl.multiple_of((2 * y + which) * 8, 8), 8), :] for y in range(4)], axis=0
    ).astype(BF16)
    res = dot(lhs, w_out[...])
    for y in range(4):
        ref[y, :, :width] = res[y * 8 : (y + 1) * 8].astype(ref.dtype)
        ref[y, :, width:] = dterms[2 * y + which].astype(ref.dtype)


def send_kernel(own_part, part1, part2, part3, w_out, dterms, send, attn):
    core = lax.axis_index("tensor") % 2
    parts = (own_part[...], part1[...], part2[...], part3[...])
    mixes, _, total = merge([read_part(x) for x in parts])
    for h in range(GROUP):
        attn[:, h * HEAD : (h + 1) * HEAD] = mixes[h] / total[:, h : h + 1]
    project_half(attn, 1 - core, w_out, dterms, send)


def keep_kernel(attn, w_out, dterms, keep):
    project_half(attn, lax.axis_index("tensor") % 2, w_out, dterms, keep)


def fold_kernel(keep, received, own_out, out1, out2, out3):
    at = lax.axis_index("tensor") // 2
    for k, ref in enumerate((own_out, out1, out2, out3)):
        block = (at + k) % 4
        ref[...] = (keep[block] + received[block].astype(F32)).astype(ref.dtype)


def final_kernel(own, in1, in2, in3, decode_out, summary_out):
    total = own[...] + in1[...].astype(F32) + in2[...].astype(F32) + in3[...].astype(F32)
    width = summary_out.shape[1]
    summary_out[...] = total[:, :width].astype(BF16)
    decode_out[0] = total[:STEPS, width:].astype(BF16)
    decode_out[1] = total[STEPS:, width:].astype(BF16)


def call(kernel, out_shape, args, scratch=(), limit=32, flops=0, smem=(), far=(), nbytes=None):
    specs = [
        pl.BlockSpec(
            memory_space=pltpu.SMEM if i in smem else pltpu.HBM if i in far else pltpu.VMEM
        )
        for i in range(len(args))
    ]
    if nbytes is None:
        nbytes = sum(math.prod(a.shape) * a.dtype.itemsize for a in args)
    outs = tuple(jax.ShapeDtypeStruct(s, d) for s, d in out_shape)
    out = pl.pallas_call(
        kernel,
        out_shape=outs,
        in_specs=specs,
        out_specs=tuple(pl.BlockSpec(memory_space=pltpu.VMEM) for _ in outs),
        scratch_shapes=list(scratch),
        compiler_params=pltpu.CompilerParams(vmem_limit_bytes=limit * MIB),
        cost_estimate=pl.CostEstimate(flops=flops, bytes_accessed=nbytes, transcendentals=0),
    )(*args)
    return out


def flip(x, axis, size, k):
    return lax.ppermute(x, axis, [(i, i ^ k) for i in range(size)])


def shift(x, axis, size, k):
    return lax.ppermute(x, axis, [(i, (i + k) % size) for i in range(size)])


def routes(step):
    return [
        (p * 8 + t, STEPS_Z[step][t % 2][p] * 8 + t) for p in range(4) for t in range(8)
    ]


def fetch(x, step):
    return lax.ppermute(x, ("path", "tensor"), [(b, a) for a, b in routes(step)])


def give_back(x, step):
    return lax.ppermute(x, ("path", "tensor"), routes(step))


def body(
    decode_in,
    path_embed,
    summary_in,
    norm_gain,
    query_gain,
    key_norm_gain,
    w_query,
    key_weight,
    w_value,
    w_out,
    key_cache,
    value_cache,
    lengths,
):
    width = w_out.shape[1]
    rows = 64
    norm_gain = norm_gain.reshape(1, -1)
    query_gain = query_gain.reshape(1, -1)
    key_gain = key_norm_gain.reshape(1, -1)

    (begun,) = call(begin_kernel, [((8, HEAD), F32)], (), flops=10**10)
    (own_rows,) = call(hold_kernel, [(summary_in.shape, BF16)], (summary_in, begun))
    across = {0: own_rows}
    for k in Y_ORDER:
        across[k] = shift(own_rows, "tensor", 8, 2 * k)
    across = [across[k] for k in range(4)]

    dterms, dkey, dvalue, cosine, sine = call(
        decode_kernel,
        [((8, 8, width // 8), BF16), ((8, HEAD), F32), ((8, HEAD), F32), ((rows, HEAD), F32), ((rows, HEAD), F32)],
        (lengths, decode_in, path_embed, norm_gain, query_gain, key_gain, w_query, key_weight,
         w_value, w_out, key_cache, value_cache),
        limit=24,
        smem=(0,),
        flops=6 * 10**9,
    )

    mine, dkey, dvalue = call(
        norm_kernel,
        [((4, 8, width), BF16), ((8, HEAD), F32), ((8, HEAD), F32)],
        (*across, norm_gain, dkey, dvalue),
    )
    other = flip(mine, "tensor", 8, 1)
    query, normed = call(
        project_kernel,
        [((rows, GROUP * HEAD), BF16), ((rows, width), BF16)],
        (mine, other, query_gain, w_query, cosine, sine),
        scratch=[pltpu.VMEM((rows, width), F32)],
        limit=24,
        flops=2 * 64 * 4096 * 512,
    )
    queries = {-1: query}
    for n in range(3):
        queries[n] = fetch(query, n)
    tails = call(
        tail_kernel,
        [((128, HEAD), BF16), ((128, HEAD), BF16)],
        (normed, key_gain, key_weight, w_value, cosine, sine, dkey, dvalue),
        limit=24,
        flops=2 * 64 * 4096 * 256,
    )

    def attend(k, after):
        (part,) = call(
            functools.partial(attend_kernel, k),
            [((rows, (GROUP + 1) * HEAD), BF16)],
            (lengths, queries[k], key_cache, value_cache, *tails, after),
            limit=24,
            smem=(0,),
            flops=3 * 10**9,
        )
        return part

    parts = []
    last = query
    for n in range(3):
        last = attend(n, last)
        parts.append(give_back(last, n))
    parts.append(attend(-1, last))

    send, attn = call(
        send_kernel,
        [((4, 8, width + width // 8), BF16), ((rows, GROUP * HEAD), F32)],
        (*parts, w_out, dterms),
        limit=24,
        flops=64 * 512 * 4096,
    )
    received = flip(send, "tensor", 8, 1)
    (keep,) = call(
        keep_kernel,
        [((4, 8, width + width // 8), F32)],
        (attn, w_out, dterms),
        limit=24,
        flops=64 * 512 * 4096,
    )
    own, out1, out2, out3 = call(
        fold_kernel,
        [((8, width + width // 8), F32)] + [((8, width + width // 8), BF16)] * 3,
        (keep, received),
    )
    outs = {1: out1, 2: out2, 3: out3}
    ins = {k: shift(outs[k], "tensor", 8, 2 * k) for k in Y_ORDER}
    decode_out, summary_out = call(
        final_kernel,
        [((2, STEPS, width // 8), BF16), ((8, width), BF16)],
        (own, ins[1], ins[2], ins[3]),
    )
    return (decode_out, summary_out)


def solution(mesh):
    in_specs = (
        P(("problem", "path"), None, None),
        P("path", None),
        P(("problem", "path", "tensor"), None),
        P(),
        P(),
        P(),
        P(None, "tensor"),
        P(None, "tensor"),
        P(None, "tensor"),
        P("tensor", None),
        P(("problem", "path"), None, "tensor"),
        P(("problem", "path"), None, "tensor"),
        P("problem"),
    )
    out_specs = (P(("problem", "path"), None, "tensor"), P(("problem", "path", "tensor"), None))
    return jax.shard_map(body, mesh=mesh, in_specs=in_specs, out_specs=out_specs, check_vma=False)
```
